256 devices in a mesh: ctx: 64 (over z, y, core), head: 4 (over x).
Axes of the slice: x: 4, y: 4, z: 8, core: 2. Of those that a mesh axis runs over, the one named last changes fastest.
Arguments:
- tokens: bfloat16 [8192, 4096], P('ctx', 'head'), may hold values from -28 to 28
- context_row: int32 [8192], replicated, may hold values from 0 to 8191, as said below
- lengths: int32 [64], replicated, may hold values from 1 to 384, 8192 in all
- q_weight: bfloat16 [4096, 4096], P('ctx', 'head'), may hold values from -0.09375 to 0.09375
- k_weight: bfloat16 [4096, 512], P('ctx', 'head'), may hold values from -0.09375 to 0.09375
- v_weight: bfloat16 [4096, 512], P('ctx', 'head'), may hold values from -0.09375 to 0.09375
- o_weight: bfloat16 [4096, 4096], P('head', 'ctx'), may hold values from -0.09375 to 0.09375
Outputs:
- layer_out: bfloat16 [8192, 4096], P('ctx', 'head')
The draws below stay inside these ranges and needn't reach their ends.
Inputs may be any that keep to these rules, and one draw needn't show every extreme that they name: `context_row`: a permutation; of the 128 loader rows of one device, at most 3 are rows of one device's 128 packed rows (rows r with the same r // 128), a number reached by some pairs of devices.
All inputs are finite; a program needn't handle non-finite values.
Results may differ from the reference program's by a relative error of at most 0.013.
The reference program's roundings to bfloat16 on the way count: a program that leaves them out, or rounds other values in their place, can miss the bound.
Values may be sent and summed in bfloat16 or wider, within the bound.
A program may use at most 64 MiB of HBM per device.

```python
import math
import jax
import jax.numpy as jnp
import numpy as np
from jax import lax

D = 4096
HEADS = 32
KV_HEADS = 4
HD = 128
TOK_DEV = 128
REACH = 3
TOKENS = 8192
DOCS = 64
DOC_MOST = 384
N_CTX = 64
N_HEAD = 4


def draw_tokens(key, part):
    key = jax.random.fold_in(key, 11)
    base_key = jax.random.fold_in(key, 0)
    result = jnp.clip(jax.random.normal(base_key, (TOKENS, D), jnp.float32), -6.0, 6.0)
    return result.astype(jnp.bfloat16)


def draw_context_row(key, part):
    key = jax.random.fold_in(key, 23)
    shift_key, label_key, send_key, recv_key = jax.random.split(key, 4)
    share = TOK_DEV // N_CTX
    device_ids = jnp.arange(N_CTX, dtype=jnp.int32)
    counts = jnp.where(device_ids % 2 == 0, 3 * share // 2, share // 2).astype(jnp.int32)
    shifts = jax.random.permutation(shift_key, N_CTX).astype(jnp.int32)
    labels = jax.random.permutation(label_key, N_CTX).astype(jnp.int32)
    label_inv = jnp.zeros((N_CTX,), jnp.int32).at[labels].set(device_ids)
    pair_group = (label_inv[None, :] - shifts[:, None]) % N_CTX
    pair_count = counts[pair_group]
    offsets = jnp.cumsum(pair_count, axis=0) - pair_count
    count_ends = jnp.cumsum(counts)
    within = jnp.arange(TOK_DEV, dtype=jnp.int32)
    group_of = jnp.sum((within[:, None] >= count_ends[None, :]).astype(jnp.int32), axis=1)
    inside = within - (count_ends - counts)[group_of]
    destination = labels[(shifts[:, None] + group_of[None, :]) % N_CTX]
    arrival = offsets[device_ids[:, None], destination] + inside[None, :]
    recv_perm = jax.vmap(lambda sub: jax.random.permutation(sub, TOK_DEV))(jax.random.split(recv_key, N_CTX)).astype(jnp.int32)
    packed_rows = destination * TOK_DEV + recv_perm[destination, arrival]
    send_perm = jax.vmap(lambda sub: jax.random.permutation(sub, TOK_DEV))(jax.random.split(send_key, N_CTX)).astype(jnp.int32)
    result = jnp.zeros((N_CTX, TOK_DEV), jnp.int32).at[device_ids[:, None], send_perm].set(packed_rows)
    return result.reshape(TOKENS)


def block_scale(key, extent, cuts, least, largest):
    def one(axis_at, blocks):
        heights = jax.random.uniform(jax.random.fold_in(jax.random.fold_in(key, 6), axis_at), (blocks,), jnp.float32, least / len(cuts), largest / len(cuts))
        return jnp.repeat(jnp.exp(heights), extent[axis_at] // blocks).reshape((-1,) + (1,) * (len(extent) - axis_at - 1))

    factor_of = one(*cuts[0])
    for cut in cuts[1:]:
        factor_of = factor_of * one(*cut)
    return factor_of


def length_profile(amount, total, reach, lean):
    weights = [(1 << 20) // math.isqrt(standing ** lean) + 1 for standing in range(2, amount + 1)]
    surplus, given = total - reach - (amount - 1), [1] * (amount - 1)
    while surplus > 0:
        candidates = [i for i in range(amount - 1) if given[i] < reach]
        mass, left = sum([weights[i] for i in candidates]), surplus
        for i in candidates:
            addition = min(reach - given[i], max(1, left * weights[i] // mass), surplus)
            given[i] = given[i] + addition
            surplus = surplus - addition
    return np.array([reach] + given)


def uneven_parts(rng, count, total, reach, lean):
    if count == 2:
        one = jax.random.randint(rng, (), max(1, total - reach), min(reach, total - 1) + 1)
        return jnp.stack([one, total - one])
    sizes = jnp.asarray(length_profile(count, total, reach, lean), jnp.int32)
    couples = (count - 1) // 2
    giver, taker = sizes[1:1 + 2 * couples:2], sizes[2:2 + 2 * couples:2]
    margin = jnp.minimum(giver - 1, reach - taker)
    passed = jax.random.randint(jax.random.fold_in(rng, 1), (couples,), 0, 1 << 20) % (margin + 1)
    sizes = sizes.at[1:1 + 2 * couples:2].set(giver - passed).at[2:2 + 2 * couples:2].set(taker + passed)
    return sizes[jax.random.permutation(jax.random.fold_in(rng, 2), count)]


def centred(stream_key, extent, scale, reach, pieces=(), held_as=jnp.bfloat16):
    level = block_scale(stream_key, extent, pieces, -0.22, 0.18) if pieces else 1.0
    values = jax.random.normal(stream_key, extent, jnp.float32) * scale * level
    return jnp.minimum(jnp.maximum(values, -reach), reach).astype(held_as)


def setup_inputs(seed: int = 0) -> dict:
    streams_of = jax.random.split(jax.random.key(seed), 8)
    tokens = draw_tokens(jax.random.fold_in(streams_of[7], 71), 0)
    context_row = draw_context_row(jax.random.fold_in(streams_of[7], 71), 0)
    lengths = uneven_parts(streams_of[2], DOCS, TOKENS, DOC_MOST, 2).astype(jnp.int32)
    q_weight = centred(streams_of[3], (D, HEADS * HD), D ** -0.5, 0.09375, ((0, 64), (1, 4)))
    k_weight = centred(streams_of[4], (D, KV_HEADS * HD), D ** -0.5, 0.09375, ((0, 64), (1, 4)))
    v_weight = centred(streams_of[5], (D, KV_HEADS * HD), D ** -0.5, 0.09375, ((0, 64), (1, 4)))
    o_weight = centred(streams_of[6], (HEADS * HD, D), (HEADS * HD) ** -0.5, 0.09375, ((0, 4), (1, 64)))
    return dict(tokens=tokens, context_row=context_row, lengths=lengths, q_weight=q_weight, k_weight=k_weight, v_weight=v_weight, o_weight=o_weight)


ROPE_BASE = 500000.0

def rotate(tensor, positions):
    half_dim = tensor.shape[-1] // 2
    frequency = ROPE_BASE ** (-jnp.arange(half_dim, dtype=jnp.float32) * 2.0 / tensor.shape[-1])
    angles = positions.astype(jnp.float32)[:, None] * frequency[None, :]
    cosine = jnp.cos(angles)[:, None, :]
    sines = jnp.sin(angles)[:, None, :]
    front_half = tensor[..., :half_dim]
    second = tensor[..., half_dim:]
    return jnp.concatenate([front_half * cosine - second * sines, second * cosine + front_half * sines], axis=-1)

def doc_layout(lengths, row_ids):
    doc_ends = jnp.cumsum(lengths)
    before = row_ids[:, None] >= doc_ends[None, :]
    doc_ids = lax.optimization_barrier(jnp.sum(before.astype(jnp.int32), axis=1))
    doc_start = lax.optimization_barrier(jnp.sum(jnp.where(before, lengths[None, :], 0), axis=1))
    return (doc_ids, row_ids - doc_start)

def reference(tokens, context_row, lengths, q_weight, k_weight, v_weight, o_weight):
    row_ids = jnp.arange(TOKENS, dtype=jnp.int32)
    source = jnp.zeros((TOKENS,), jnp.int32).at[context_row].set(row_ids)
    placed = tokens[source]
    doc_ids, position = doc_layout(lengths, row_ids)
    q_heads = rotate(jnp.dot(placed, q_weight, preferred_element_type=jnp.float32).reshape(TOKENS, HEADS, HD), position).astype(jnp.bfloat16)
    key_rows = rotate(jnp.dot(placed, k_weight, preferred_element_type=jnp.float32).reshape(TOKENS, KV_HEADS, HD), position).astype(jnp.bfloat16)
    value_rows = jnp.dot(placed, v_weight, preferred_element_type=jnp.float32).astype(jnp.bfloat16).reshape(TOKENS, KV_HEADS, HD)
    span = REACH * TOK_DEV
    width_keys = span + TOK_DEV
    keys_pad = jnp.concatenate([jnp.zeros((span, KV_HEADS, HD), jnp.bfloat16), key_rows], axis=0)
    values_pad = jnp.concatenate([jnp.zeros((span, KV_HEADS, HD), jnp.bfloat16), value_rows], axis=0)
    docs_pad = jnp.concatenate([jnp.full((span,), -1, jnp.int32), doc_ids], axis=0)
    group_size = HEADS // KV_HEADS
    factor = 1.0 / math.sqrt(HD)

    def attend_block(block_index):
        begin = (block_index * TOK_DEV).astype(jnp.int32)
        query_block = lax.dynamic_slice_in_dim(q_heads, begin, TOK_DEV, 0).astype(jnp.float32).reshape(TOK_DEV, KV_HEADS, group_size, HD)
        key_block = lax.dynamic_slice_in_dim(keys_pad, begin, width_keys, 0).astype(jnp.float32)
        value_block = lax.dynamic_slice_in_dim(values_pad, begin, width_keys, 0).astype(jnp.float32)
        query_docs = lax.dynamic_slice_in_dim(doc_ids, begin, TOK_DEV, 0)
        key_docs = lax.dynamic_slice_in_dim(docs_pad, begin, width_keys, 0)
        query_ids = begin + jnp.arange(TOK_DEV, dtype=jnp.int32)
        key_ids = begin - span + jnp.arange(width_keys, dtype=jnp.int32)
        allowed = (query_docs[:, None] == key_docs[None, :]) & (key_ids[None, :] <= query_ids[:, None])
        scores = jnp.einsum('qkgd,skd->kgqs', query_block, key_block) * factor
        scores = jnp.where(allowed[None, None], scores, -jnp.inf)
        row_top = lax.optimization_barrier(jnp.max(scores, axis=-1, keepdims=True))
        weighting = jnp.exp(scores - row_top)
        denominator = lax.optimization_barrier(jnp.sum(weighting, axis=-1))
        rounded = lax.optimization_barrier(weighting.astype(jnp.bfloat16)).astype(jnp.float32)
        summed = jnp.einsum('kgqs,skd->kgqd', rounded, value_block) / denominator[..., None]
        return jnp.transpose(summed, (2, 0, 1, 3)).reshape(TOK_DEV, HEADS * HD).astype(jnp.bfloat16)
    attended = lax.map(attend_block, jnp.arange(N_CTX, dtype=jnp.int32)).reshape(TOKENS, HEADS * HD)
    share = HEADS * HD // N_HEAD
    running = jnp.zeros((TOKENS, D), jnp.float32)
    for group_index in range(N_HEAD):
        partial_g = jnp.dot(attended[:, group_index * share:(group_index + 1) * share], o_weight[group_index * share:(group_index + 1) * share], preferred_element_type=jnp.float32)
        running = running + lax.optimization_barrier(partial_g.astype(jnp.bfloat16)).astype(jnp.float32)
    return running.astype(jnp.bfloat16)
```

```python
import math

import jax
import jax.numpy as jnp
from jax import lax
from jax.experimental import pallas as pl
from jax.experimental.pallas import tpu as pltpu
from jax.sharding import PartitionSpec as P

MESH = pl.DeviceIdType.MESH
F32 = jnp.float32
BF16 = jnp.bfloat16
ROPE_BASE = 500000.0
HD = 128

DZ = (0, 1, -1, 2, -2, 3, -3, 4)
DY = (0, 1, -1, 2)
ZS = {d: i for i, d in enumerate(DZ)}
YS = {d: i for i, d in enumerate(DY)}
GROUPS = ((0, 1), (1, 3), (3, 5), (5, 7), (7, 8))

LINK_RATE, LINK_LATENCY = 47.0, 2.0
PEER_RATE, PEER_LATENCY = 400.0, 1.0


class Message:
    def __init__(self, name, link, src, dst, deps, size, prio):
        self.name, self.link, self.src, self.dst = name, link, src, dst
        self.deps, self.size, self.prio = deps, size, prio


def gather_messages(tag, rows, width1, width2, ready, rank):
    out = []
    half = rows // 2
    size1 = rows * width1 * 2e-3
    size2 = rows * width2 * 2e-3
    full, top, bottom = (0, rows), (0, half), (half, half)

    def one(dz, dy, part):
        return (tag + "1", ZS[dz], YS[dy], part)

    def pair(dz, which):
        return (tag + "1", ZS[dz], (2 * which, 2), full)

    def two(dy, dz, part):
        return (tag + "2", YS[dy], ZS[dz], part)

    def group(dy, g):
        lo, hi = GROUPS[g]
        return (tag + "2", YS[dy], (lo, hi - lo), full)

    def add(name, link, src, dst, deps, size, prio):
        out.append(Message(tag + name, link, src, dst, [tag + d for d in deps] + ready, size, (rank,) + prio))

    add("1y+1", "+y", one(0, 0, full), one(0, -1, full), [], size1, (0, 1))
    add("1y-1", "-y", one(0, 0, full), one(0, 1, full), [], size1, (0, 1))
    add("1y+2", "+y", one(0, -1, top), one(0, 2, top), ["1y+1"], size1 / 2, (0, 2))
    add("1y-2", "-y", one(0, 1, bottom), one(0, 2, bottom), ["1y-1"], size1 / 2, (0, 2))
    first = {0: ["1y-1"], 1: ["1y+1", "1y+2", "1y-2"]}
    for which in (0, 1):
        for sign, link in ((1, "+z"), (-1, "-z")):
            mark = "+" if sign > 0 else "-"
            for step in (1, 2, 3, 4):
                if step == 4 and (sign > 0) != (which == 0):
                    continue
                deps = first[which] if step == 1 else [f"1z{which}{mark}{step - 1}"]
                far = 4 if step == 4 else -sign * step
                add(f"1z{which}{mark}{step}", link, pair(-sign * (step - 1), which), pair(far, which), deps,
                    2 * size1, (1, step))
    for sign, link in ((1, "+z"), (-1, "-z")):
        mark = "+" if sign > 0 else "-"
        for step in (1, 2, 3, 4):
            deps = [] if step == 1 else [f"2z{mark}{step - 1}"]
            part = full if step < 4 else (top if sign > 0 else bottom)
            far = 4 if step == 4 else -sign * step
            add(f"2z{mark}{step}", link, two(0, -sign * (step - 1), part), two(0, far, part), deps,
                size2 if step < 4 else size2 / 2, (0, step))
    for g, (lo, hi) in enumerate(GROUPS):
        deps = [] if g == 0 else [f"2z+{g}", f"2z-{g}"]
        amount = size2 * (hi - lo)
        add(f"2y{g}+1", "+y", group(0, g), group(-1, g), deps, amount, (1, g))
        add(f"2y{g}-1", "-y", group(0, g), group(1, g), deps, amount, (1, g))
        if g % 2 == 0:
            add(f"2y{g}+2", "+y", group(-1, g), group(2, g), [f"2y{g}+1"], amount, (1, g))
        else:
            add(f"2y{g}-2", "-y", group(1, g), group(2, g), [f"2y{g}-1"], amount, (1, g))
    return out


def needs(tag, dz):
    g = [i for i, (lo, hi) in enumerate(GROUPS) if lo <= ZS[dz] < hi][0]
    far = f"2y{g}+2" if g % 2 == 0 else f"2y{g}-2"
    names = [f"2y{g}+1", f"2y{g}-1", far]
    if dz == 0:
        names += ["1y+1", "1y-1", "1y+2", "1y-2"]
    elif dz == 4:
        names += ["1z0+4", "1z1-4", "2z+4", "2z-4"]
    else:
        mark, step = ("+" if dz < 0 else "-"), abs(dz)
        names += [f"1z0{mark}{step}", f"1z1{mark}{step}", f"2z{mark}{step}"]
    return [tag + n for n in names]


def all_messages():
    out = [
        Message("w1", "peer", None, None, [], 33, (0,)),
        Message("w2", "peer", None, None, [], 50, (0,)),
        Message("xs", "peer", None, None, [], 262, (0,)),
        Message("x+", "+x", None, None, [], 262, (0,)),
        Message("x-", "-x", None, None, [], 262, (0,)),
        Message("x+2", "+x", None, None, ["x+"], 131, (1,)),
        Message("x-2", "-x", None, None, ["x-"], 131, (1,)),
        Message("xs+", "peer", None, None, ["x+"], 262, (1,)),
        Message("xs-", "peer", None, None, ["x-"], 262, (1,)),
        Message("xs2", "peer", None, None, ["x+2", "x-2"], 262, (1,)),
    ]
    out += gather_messages("q", 128, 256, 384, ["w1", "w2"], 0)
    out += gather_messages("o", 64, 384, 640, [], 1)
    return out


def simulate(messages):
    free, arrival, start = {}, {}, {}
    pending = list(messages)
    while pending:
        best = None
        by_link = {}
        for m in pending:
            if all(d in arrival for d in m.deps):
                at = max([arrival[d] for d in m.deps], default=0.0)
                by_link.setdefault(m.link, []).append((at, m))
        for link, options in by_link.items():
            begin = max(free.get(link, 0.0), min(at for at, _ in options))
            at, m = min(((at, m) for at, m in options if at <= begin), key=lambda p: p[1].prio)
            if best is None or begin < best[0]:
                best = (begin, m, at)
        begin, m, at = best
        peer = m.link == "peer"
        span = m.size / (PEER_RATE if peer else LINK_RATE)
        free[m.link] = begin + span
        arrival[m.name] = begin + span + (PEER_LATENCY if peer else LINK_LATENCY)
        start[m.name] = max(at, begin - 3.0)
        pending.remove(m)
    return start, arrival


HALO = ["halo"]
ATTEND = [f"att{qb}{pair}" for qb in (0, 1) for pair in (0, 1)]


def steps_of():
    x_all = ["x+", "x-", "xs", "xs+", "xs-", "xs2"]
    steps = [("tables", [], 1.5)]
    steps += [(f"q{dz}", needs("q", dz) + x_all + ["tables"], 0.6) for dz in DZ]
    steps += [("kv", [f"q{dz}" for dz in DZ], 0.5), ("rope", ["kv"], 1.0), ("halo", ["kv"], 0.5)]
    steps += [(name, ["halo", "rope"], 1.0) for name in ATTEND]
    steps += [("attsend0", ATTEND[:2], 0.1), ("attsend1", ATTEND[2:], 0.1)]
    steps += [("attget", ["attsend0", "attsend1"], 0.1)]
    steps += [(f"o{dz}", needs("o", dz) + ["attget"], 0.5) for dz in DZ]
    return steps


def plan():
    messages = all_messages()
    start, arrival = simulate(messages)
    actions = [(start[m.name], 1, "send", m.name) for m in messages]
    actions += [(arrival[m.name], 0, "recv", m.name) for m in messages]
    actions.sort()
    steps = steps_of()
    halo_from = {"halo": 4.0, "attget": 1.0}
    done, finished, order, clock = set(), {}, [], 0.0
    waiting = list(steps)
    index = 0
    while index < len(actions) or waiting:
        ready = None
        for step in waiting:
            if all(d in done for d in step[1]):
                late = max([finished.get(d, 0.0) for d in step[1]], default=0.0) + halo_from.get(step[0], 0.0)
                if index >= len(actions) or max(clock, late) <= actions[index][0] - 0.1:
                    ready = (step, late)
                    break
        if ready is not None:
            step, late = ready
            order.append(("step", step[0]))
            clock = max(clock, late) + step[2]
            finished[step[0]] = clock
            done.add(step[0])
            waiting.remove(step)
            continue
        at, _, kind, name = actions[index]
        index += 1
        order.append((kind, name))
        clock = max(clock, at) + 0.1
        if kind == "recv":
            done.add(name)
    return messages, order, max(arrival.values())


def kernel(messages, order, placed, lens, qw, kw, vw, ow, out,
           q1, q2, o1, o2, st1, st2, xs, acc1, acc2, cs, bias, qs, kv, vt, att, part, rs,
           send, recv, hsend, hrecv, asend, arecv, psend, precv):
    ctx, x = lax.axis_index("ctx"), lax.axis_index("head")
    z, y, core = ctx // 8, (ctx // 2) % 4, ctx % 2
    chip = ctx // 2
    other = 1 - core
    buffers = {"q1": q1, "q2": q2, "o1": o1, "o2": o2}
    number = {m.name: i for i, m in enumerate(messages)}

    def at(dz, dy, which, dx=0):
        return ((lax.rem(z + dz + 8, 8) * 4 + lax.rem(y + dy + 4, 4)) * 2 + which, lax.rem(x + dx + 4, 4))

    def chip_at(by, which):
        return (lax.rem(chip + by + 32, 32) * 2 + which, x)

    peers = [at(1, 0, core), at(-1, 0, core), at(0, 1, core), at(0, -1, core), at(0, 0, other)]
    peers += [at(0, 0, which, dx) for dx in (1, 2, 3) for which in (0, 1)]
    peers += [chip_at(by, which) for by in (1, 2, -1, -2) for which in (0, 1)]
    barrier = pltpu.get_barrier_semaphore()
    for peer in peers:
        pl.semaphore_signal(barrier, inc=1, device_id=peer, device_id_type=MESH)

    for d in (0, 1):
        st1[d] = qw[:, 512 * d : 512 * d + 256]
        st2[d, :, :256] = qw[:, 512 * d + 256 : 512 * d + 512]
        st2[d, :, 256:] = (kw if d == 0 else vw)[...]
    mine = pl.ds(pl.multiple_of(core * 64, 64), 64)
    theirs = pl.ds(pl.multiple_of(other * 64, 64), 64)
    q1[0, 0, mine] = st1[core]
    q2[0, 0, mine] = st2[core]
    xs[x, core] = placed[...]
    eye = (
        lax.broadcasted_iota(jnp.int32, (64, 64), 0) == lax.broadcasted_iota(jnp.int32, (64, 64), 1)
    ).astype(F32).astype(BF16)
    turned = lax.dot_general(eye, ow[...], (((1,), (1,)), ((), ())), preferred_element_type=F32).astype(BF16)
    o1[0, 0] = turned[:, :384]
    o2[0, 0] = turned[:, 384:]
    pl.semaphore_wait(barrier, len(peers))

    x_low, x_high, x_far = lax.rem(x + 3, 4), lax.rem(x + 1, 4), lax.rem(x + 2, 4)
    top, bottom = pl.ds(0, 64), pl.ds(64, 64)
    across = at(0, 0, other)
    special = {
        "w1": (st1.at[other], q1.at[0, 0, mine], q1.at[0, 0, theirs], across),
        "w2": (st2.at[other], q2.at[0, 0, mine], q2.at[0, 0, theirs], across),
        "xs": (xs.at[x, core], xs.at[x, core], xs.at[x, other], across),
        "x+": (xs.at[x, core], xs.at[x, core], xs.at[x_low, core], at(0, 0, core, 1)),
        "x-": (xs.at[x, core], xs.at[x, core], xs.at[x_high, core], at(0, 0, core, -1)),
        "x+2": (xs.at[x_low, core, top], xs.at[x_low, core, top], xs.at[x_far, core, top], at(0, 0, core, 1)),
        "x-2": (xs.at[x_high, core, bottom], xs.at[x_high, core, bottom], xs.at[x_far, core, bottom],
                at(0, 0, core, -1)),
        "xs+": (xs.at[x_low, core], xs.at[x_low, core], xs.at[x_low, other], across),
        "xs-": (xs.at[x_high, core], xs.at[x_high, core], xs.at[x_high, other], across),
        "xs2": (xs.at[x_far, core], xs.at[x_far, core], xs.at[x_far, other], across),
    }
    to = {"+z": at(1, 0, core), "-z": at(-1, 0, core), "+y": at(0, 1, core), "-y": at(0, -1, core)}

    def view(place):
        name, a, b, (lo, n) = place
        b = pl.ds(*b) if isinstance(b, tuple) else b
        return buffers[name].at[a, b, pl.ds(lo, n)]

    def remote(src, dst, ssem, rsem, device):
        return pltpu.make_async_remote_copy(
            src_ref=src, dst_ref=dst, send_sem=ssem, recv_sem=rsem, device_id=device, device_id_type=MESH
        )

    def copy_of(m, coming=False):
        i = number[m.name]
        if m.name in special:
            src, dst, land, device = special[m.name]
        else:
            src, dst, land, device = view(m.src), view(m.dst), view(m.dst), to[m.link]
        if coming:
            src = dst = land
        return remote(src, dst, send.at[i], recv.at[i], device)

    by_name = {m.name: m for m in messages}

    def tables():
        base = chip * 256
        i0 = lax.broadcasted_iota(jnp.int32, (64, 64), 0)
        i1 = lax.broadcasted_iota(jnp.int32, (64, 64), 1)
        spread = jnp.broadcast_to(lens[...].astype(F32), (64, 64))
        end_col = jnp.sum(jnp.where(i1 <= i0, spread, 0.0), axis=1, keepdims=True)
        len_col = jnp.sum(jnp.where(i1 == i0, spread, 0.0), axis=1, keepdims=True)
        end_row = jnp.sum(jnp.where(i0 <= i1, jnp.broadcast_to(len_col, (64, 64)), 0.0), axis=0, keepdims=True)
        row_id = (base + lax.broadcasted_iota(jnp.int32, (64, 256), 1)).astype(F32)
        before = row_id >= end_col
        q_doc = jnp.sum(jnp.where(before, 1.0, 0.0), axis=0, keepdims=True)
        position = row_id - jnp.sum(jnp.where(before, len_col, 0.0), axis=0, keepdims=True)
        turn = lax.broadcasted_iota(jnp.int32, (64, 256), 0).astype(F32)
        angle = position * jnp.exp(turn * (-2.0 / HD * math.log(ROPE_BASE)))
        cs[...] = jnp.transpose(jnp.concatenate([jnp.cos(angle), jnp.sin(angle)], axis=0))
        key_id = base - 384 + lax.broadcasted_iota(jnp.int32, (640, 64), 0)
        k_doc = jnp.sum(jnp.where(key_id.astype(F32) >= end_row, 1.0, 0.0), axis=1, keepdims=True)
        for qb in (0, 1):
            lo = 128 * qb
            kid = base - 384 + lo + lax.broadcasted_iota(jnp.int32, (512, 128), 0)
            qid = base + lo + lax.broadcasted_iota(jnp.int32, (512, 128), 1)
            allowed = (k_doc[lo : lo + 512] == q_doc[:, lo : lo + 128]) & (kid <= qid) & (kid >= 0)
            bias[qb] = jnp.where(allowed, 0.0, -jnp.inf)

    def columns_of(dz):
        zz = lax.rem(z + dz + 8, 8)
        parts = []
        for dy in DY:
            lane = pl.multiple_of((lax.rem(zz, 2) * 4 + lax.rem(y + dy + 4, 4)) * 128, 128)
            parts.append(xs[zz // 2, :, :, pl.ds(lane, 128)].reshape(256, 128))
        return jnp.concatenate(parts, axis=1)

    def project(dz):
        s = ZS[dz]
        lhs = columns_of(dz)
        one = jnp.dot(lhs, q1[s].reshape(512, 256), preferred_element_type=F32)
        two = jnp.dot(lhs, q2[:, s].reshape(512, 384), preferred_element_type=F32)
        if dz == 0:
            acc1[...] = one
            acc2[...] = two
        else:
            acc1[...] += one
            acc2[...] += two

    def turned_pairs():
        table = cs[...]
        swapped = pltpu.roll(table, 64, 1)
        low = lax.broadcasted_iota(jnp.int32, (256, 128), 1) < 64
        return jnp.where(low, table, swapped), jnp.where(low, -swapped, table)

    def rope(e):
        cosine, sine = turned_pairs()
        return e * cosine + pltpu.roll(e, 64, 1) * sine

    halo = [
        (0, core, pl.ds(384, 256), pl.ds(384, 256), across),
        (1, 0, pl.ds(384, 256), pl.ds(128, 256), chip_at(1, 0)),
        (2, 0, pl.ds(384, 256), pl.ds(128, 256), chip_at(1, 1)),
        (3, 0, pl.ds(512, 128), pl.ds(0, 128), chip_at(2, 0)),
        (4, 0, pl.ds(512, 128), pl.ds(0, 128), chip_at(2, 1)),
    ]

    def halo_copy(i):
        kind, _, src, dst, device = halo[i]
        return remote(kv.at[core, src], kv.at[core, dst], hsend.at[i], hrecv.at[core, (kind + 1) // 2], device)

    def make_kv():
        raw = acc2[:, 256:384]
        kv[core, 384:640] = jnp.where(core == 0, rope(raw), raw).astype(BF16)
        for i in range(5):
            halo_copy(i).start()

    def rope_queries():
        for h in range(4):
            e = acc1[:, 128 * h : 128 * h + 128] if h < 2 else acc2[:, 128 * (h - 2) : 128 * (h - 2) + 128]
            turned_e = rope(e).astype(BF16)
            for qb in (0, 1):
                qs[qb, h // 2, 128 * (h % 2) : 128 * (h % 2) + 128] = turned_e[128 * qb : 128 * qb + 128]

    def wait_halo():
        remote(kv.at[other, pl.ds(384, 256)], kv.at[other, pl.ds(384, 256)], hsend.at[0],
               hrecv.at[other, 0], across).wait_recv()
        for c in (0, 1):
            remote(kv.at[c, pl.ds(128, 256)], kv.at[c, pl.ds(128, 256)], hsend.at[1], hrecv.at[c, 1],
                   across).wait_recv()
            remote(kv.at[c, pl.ds(0, 128)], kv.at[c, pl.ds(0, 128)], hsend.at[3], hrecv.at[c, 2],
                   across).wait_recv()
        eye = (
            lax.broadcasted_iota(jnp.int32, (128, 128), 0) == lax.broadcasted_iota(jnp.int32, (128, 128), 1)
        ).astype(F32).astype(BF16)
        vt[...] = lax.dot_general(eye, kv[1], (((1,), (1,)), ((), ())), preferred_element_type=F32).astype(BF16)

    def attend(qb, pair):
        keys = kv[0, 128 * qb : 128 * qb + 512]
        scores = lax.dot_general(keys, qs[qb, pair], (((1,), (1,)), ((), ())), preferred_element_type=F32)
        mask = bias[qb]
        scores = scores * (1.0 / math.sqrt(HD)) + jnp.concatenate([mask, mask], axis=1)
        expo = jnp.exp(scores - jnp.max(scores, axis=0, keepdims=True))
        denominator = jnp.sum(expo, axis=0, keepdims=True)
        summed = jnp.dot(vt[:, 128 * qb : 128 * qb + 512], expo.astype(BF16), preferred_element_type=F32)
        result = (summed / denominator).astype(BF16)
        for h in (0, 1):
            att[core, qb, 128 * (2 * pair + h) : 128 * (2 * pair + h) + 128] = result[:, 128 * h : 128 * h + 128]

    def att_copy(qb):
        return remote(att.at[core, qb], att.at[core, qb], asend.at[qb], arecv.at[qb], across)

    def wait_att():
        for qb in (0, 1):
            remote(att.at[other, qb], att.at[other, qb], asend.at[qb], arecv.at[qb], across).wait_recv()

    def part_copy(dz, t, start):
        s = ZS[dz]
        zz = lax.rem(z + dz + 8, 8)
        goal = zz // 2
        here = (goal == x) & (core == t)
        sem = precv.at[core, x, lax.rem(zz, 2)]
        land = rs.at[core, x, lax.rem(zz, 2)]

        @pl.when(jnp.logical_not(here))
        def _():
            copy = remote(part.at[s, t], land, psend.at[s, t], sem, (chip * 2 + t, goal))
            copy.start() if start else copy.wait_send()

        if start:

            @pl.when(here)
            def _():
                pltpu.make_async_copy(part.at[s, t], land, sem).start()

    def out_project(dz):
        s = ZS[dz]
        weights = jnp.concatenate([att[:, 0].reshape(1024, 128), att[:, 1].reshape(1024, 128)], axis=1)
        total = jnp.dot(o1[s].reshape(256, 384), weights[:384], preferred_element_type=F32)
        total += jnp.dot(o2[:, s].reshape(256, 640), weights[384:], preferred_element_type=F32)
        total = total.astype(BF16)
        for t in (0, 1):
            part[s, t] = total[:, 128 * t : 128 * t + 128]
            part_copy(dz, t, True)

    def run(name):
        if name == "tables":
            tables()
        elif name == "kv":
            make_kv()
        elif name == "rope":
            rope_queries()
        elif name == "halo":
            wait_halo()
        elif name == "attget":
            wait_att()
        elif name.startswith("attsend"):
            att_copy(int(name[7])).start()
        elif name.startswith("att"):
            attend(int(name[3]), int(name[4]))
        elif name.startswith("q"):
            project(int(name[1:]))
        else:
            out_project(int(name[1:]))

    for kind, name in order:
        if kind == "send":
            copy_of(by_name[name]).start()
        elif kind == "recv":
            copy_of(by_name[name], True).wait_recv()
        else:
            run(name)

    for m in messages:
        copy_of(m).wait_send()
    for i in range(5):
        halo_copy(i).wait_send()
    for qb in (0, 1):
        att_copy(qb).wait_send()
    for dz in DZ:
        for t in (0, 1):
            part_copy(dz, t, False)
    for zz in (0, 1):
        sums = []
        for c in (0, 1):
            total = None
            for g in range(4):
                land = rs.at[c, g, zz]
                remote(land, land, psend.at[0, 0], precv.at[c, g, zz], across).wait_recv()
                term = rs[c, g, zz].astype(F32)
                total = term if total is None else total + term
            sums.append(total)
        for dy in DY:
            s = YS[dy]
            block = jnp.concatenate([sums[0][64 * s : 64 * s + 64], sums[1][64 * s : 64 * s + 64]], axis=0)
            lane = pl.multiple_of((zz * 4 + lax.rem(y + dy + 4, 4)) * 128, 128)
            out[:, pl.ds(lane, 128)] = jnp.transpose(block).astype(BF16)


def fused(placed, lengths, qw, kw, vw, ow):
    messages, order, _ = plan()
    count = len(messages)
    dma = pltpu.SemaphoreType.DMA
    scratch = [
        pltpu.VMEM((8, 4, 128, 256), BF16),
        pltpu.VMEM((4, 8, 128, 384), BF16),
        pltpu.VMEM((8, 4, 64, 384), BF16),
        pltpu.VMEM((4, 8, 64, 640), BF16),
        pltpu.VMEM((2, 64, 256), BF16),
        pltpu.VMEM((2, 64, 384), BF16),
        pltpu.VMEM((4, 2, 128, 1024), BF16),
        pltpu.VMEM((256, 256), F32),
        pltpu.VMEM((256, 384), F32),
        pltpu.VMEM((256, 128), F32),
        pltpu.VMEM((2, 512, 128), F32),
        pltpu.VMEM((2, 2, 256, 128), BF16),
        pltpu.VMEM((2, 640, 128), BF16),
        pltpu.VMEM((128, 640), BF16),
        pltpu.VMEM((2, 2, 512, 128), BF16),
        pltpu.VMEM((8, 2, 256, 128), BF16),
        pltpu.VMEM((2, 4, 2, 256, 128), BF16),
        dma((count,)),
        dma((count,)),
        dma((5,)),
        dma((2, 3)),
        dma((2,)),
        dma((2,)),
        dma((8, 2)),
        dma((2, 4, 2)),
    ]

    def body(*refs):
        kernel(messages, order, *refs)

    return pl.pallas_call(
        body,
        out_shape=jax.ShapeDtypeStruct((128, 1024), BF16),
        in_specs=[pl.BlockSpec(memory_space=pltpu.VMEM)] * 6,
        out_specs=pl.BlockSpec(memory_space=pltpu.VMEM),
        scratch_shapes=scratch,
        compiler_params=pltpu.CompilerParams(
            collective_id=0, has_side_effects=True, vmem_limit_bytes=48 * 2**20
        ),
    )(placed, lengths.reshape(1, 64), qw, kw, vw, ow)


def relayout(tokens, context_row, this_dev, devices):
    rows_dev, width = tokens.shape
    cap = 3
    table = context_row.reshape(devices, rows_dev)
    own = lax.dynamic_slice_in_dim(context_row, this_dev * rows_dev, rows_dev)
    target = own // rows_dev
    row = jnp.arange(rows_dev, dtype=jnp.int32)
    rank = jnp.sum((target[:, None] == target[None, :]) & (row[None, :] < row[:, None]), axis=1, dtype=jnp.int32)
    slot = target * cap + rank
    pick = (jnp.arange(devices * cap, dtype=jnp.int32)[:, None] == slot[None, :]).astype(BF16)
    outgoing = jnp.dot(pick, tokens, preferred_element_type=F32).astype(BF16)
    arrived = lax.all_to_all(
        outgoing.reshape(devices, cap, width), "ctx", split_axis=0, concat_axis=0, tiled=True
    ).reshape(devices * cap, width)
    here = table // rows_dev == this_dev
    upper = (row[:, None] < row[None, :]).astype(BF16)
    order = jnp.dot(here.astype(BF16), upper, preferred_element_type=F32).astype(jnp.int32)
    landing = jnp.stack(
        [jnp.sum(jnp.where(here & (order == j), table % rows_dev + 1, 0), axis=1) - 1 for j in range(cap)], axis=1
    ).reshape(-1)
    place = (row[:, None] == landing[None, :]).astype(BF16)
    return jnp.dot(place, arrived, preferred_element_type=F32).astype(BF16)


def per_device(tokens, context_row, lengths, qw, kw, vw, ow):
    placed = relayout(tokens, context_row, lax.axis_index("ctx"), lax.axis_size("ctx"))
    return fused(placed, lengths, qw, kw, vw, ow)


def solution(mesh):
    return jax.shard_map(
        per_device,
        mesh=mesh,
        in_specs=(
            P("ctx", "head"),
            P(),
            P(),
            P("ctx", "head"),
            P("ctx", "head"),
            P("ctx", "head"),
            P("head", "ctx"),
        ),
        out_specs=P("ctx", "head"),
        check_vma=False,
    )
```

```python
import math

import jax
import jax.numpy as jnp
from jax import lax
from jax.experimental import pallas as pl
from jax.experimental.pallas import tpu as pltpu
from jax.sharding import PartitionSpec as P

MESH = pl.DeviceIdType.MESH
F32 = jnp.float32
BF16 = jnp.bfloat16
ROPE_BASE = 500000.0
HD = 128

DZ = (0, 1, -1, 2, -2, 3, -3, 4)
DY = (0, 1, -1, 2)
ZS = {d: i for i, d in enumerate(DZ)}
YS = {d: i for i, d in enumerate(DY)}
GROUPS = ((0, 1), (1, 3), (3, 5), (5, 7), (7, 8))
WIDE_GROUPS = ((0, 3), (3, 7), (7, 8))

LINK_RATE, LINK_LATENCY = 47.0, 2.4
PEER_RATE, PEER_LATENCY = 400.0, 1.0
AHEAD = 1.0


class Node:
    def __init__(self, name, link, deps, size, prio=(0,), src=None, dst=None):
        self.name, self.link, self.deps, self.size, self.prio = name, link, deps, size, prio
        self.src, self.dst = src, dst


def gather_messages(tag, rows, width1, width2, ready, rank, groups=GROUPS):
    out = []
    half = rows // 2
    size1 = rows * width1 * 2e-3
    size2 = rows * width2 * 2e-3
    full, top, bottom = (0, rows), (0, half), (half, half)

    def one(dz, dy, part):
        return (tag + "1", ZS[dz], YS[dy], part)

    def pair(dz, which):
        return (tag + "1", ZS[dz], (2 * which, 2), full)

    def two(dy, dz, part):
        return (tag + "2", YS[dy], ZS[dz], part)

    def group(dy, g):
        lo, hi = groups[g]
        return (tag + "2", YS[dy], (lo, hi - lo), full)

    def add(name, link, src, dst, deps, size, prio):
        out.append(Node(tag + name, link, [tag + d for d in deps] + ready, size, (rank,) + prio, src, dst))

    if width1:
        add("1y+1", "+y", one(0, 0, full), one(0, -1, full), [], size1, (0, 1))
        add("1y-1", "-y", one(0, 0, full), one(0, 1, full), [], size1, (0, 1))
        add("1y+2", "+y", one(0, -1, top), one(0, 2, top), ["1y+1"], size1 / 2, (0, 2))
        add("1y-2", "-y", one(0, 1, bottom), one(0, 2, bottom), ["1y-1"], size1 / 2, (0, 2))
    first = {0: ["1y-1"], 1: ["1y+1", "1y+2", "1y-2"]}
    for which in (0, 1) if width1 else ():
        for sign, link in ((1, "+z"), (-1, "-z")):
            mark = "+" if sign > 0 else "-"
            for step in (1, 2, 3, 4):
                if step == 4 and (sign > 0) != (which == 0):
                    continue
                deps = first[which] if step == 1 else [f"1z{which}{mark}{step - 1}"]
                far = 4 if step == 4 else -sign * step
                add(f"1z{which}{mark}{step}", link, pair(-sign * (step - 1), which), pair(far, which), deps,
                    2 * size1, (1, step))
    for sign, link in ((1, "+z"), (-1, "-z")):
        mark = "+" if sign > 0 else "-"
        for step in (1, 2, 3, 4):
            deps = [] if step == 1 else [f"2z{mark}{step - 1}"]
            part = full if step < 4 else (top if sign > 0 else bottom)
            far = 4 if step == 4 else -sign * step
            add(f"2z{mark}{step}", link, two(0, -sign * (step - 1), part), two(0, far, part), deps,
                size2 if step < 4 else size2 / 2, (0, step))
    for g, (lo, hi) in enumerate(groups):
        deps = []
        for dz in DZ[lo:hi]:
            deps += z_messages(dz)
        amount = size2 * (hi - lo)
        add(f"2y{g}+1", "+y", group(0, g), group(-1, g), deps, amount, (1, g))
        add(f"2y{g}-1", "-y", group(0, g), group(1, g), deps, amount, (1, g))
        if g % 2 == 0:
            add(f"2y{g}+2", "+y", group(-1, g), group(2, g), [f"2y{g}+1"], amount, (1, g))
        else:
            add(f"2y{g}-2", "-y", group(1, g), group(2, g), [f"2y{g}-1"], amount, (1, g))
    return out


def z_messages(dz):
    if dz == 0:
        return []
    return ["2z+4", "2z-4"] if dz == 4 else [f"2z{'+' if dz < 0 else '-'}{abs(dz)}"]


def needs(tag, dz, which, groups=GROUPS):
    g = [i for i, (lo, hi) in enumerate(groups) if lo <= ZS[dz] < hi][0]
    if which == 0:
        names = z_messages(dz) + [f"2y{g}-1"]
    else:
        names = [f"2y{g}+1", f"2y{g}+2" if g % 2 == 0 else f"2y{g}-2"]
    if tag != "k":
        if dz == 0:
            names += ["1y-1"] if which == 0 else ["1y+1", "1y+2", "1y-2"]
        elif dz == 4:
            names += ["1z0+4"] if which == 0 else ["1z1-4"]
        else:
            names += [f"1z{which}{'+' if dz < 0 else '-'}{abs(dz)}"]
    return [tag + n for n in names]


def all_nodes():
    x_all = ["x+a", "x+b", "x-a", "x-b", "xs+", "xs-", "xs2"]
    nodes = [
        Node("w1", "peer", [], 33),
        Node("w2", "peer", [], 33),
        Node("w3", "peer", [], 17),
        Node("r+z", "+z", [], 384, (-2,)),
        Node("r-z", "-z", [], 384, (-2,)),
        Node("r+y", "+y", [], 192, (-2,)),
        Node("r-y", "-y", [], 192, (-2,)),
        Node("rows", "peer", ["r+z", "r-z", "r+y", "r-y"], 384, (-1,)),
        Node("x+a", "+x", ["place"], 131, (0, 0)),
        Node("x+b", "+x", ["place"], 131, (0, 1)),
        Node("x-b", "-x", ["place"], 131, (0, 0)),
        Node("x-a", "-x", ["place"], 131, (0, 1)),
        Node("x+2", "+x", ["x+a"], 131, (0, 2)),
        Node("x-2", "-x", ["x-b"], 131, (0, 2)),
        Node("xs+", "peer", ["x+a", "x+b"], 262, (1,)),
        Node("xs-", "peer", ["x-a", "x-b"], 262, (1,)),
        Node("xs2", "peer", ["x+2", "x-2"], 262, (1,)),
        Node("h0", "peer", ["kv"], 65, (0,)),
        Node("h1", "+y", ["kv"], 85, (-1, 0)),
        Node("h2", "+y", ["kv"], 65, (-1, 1)),
        Node("h1s", "peer", ["h1"], 65, (0,)),
        Node("h2s", "peer", ["h2"], 33, (0,)),
    ]
    nodes += gather_messages("k", 128, 0, 128, ["w3"], 0, WIDE_GROUPS)
    nodes += gather_messages("q", 128, 256, 256, ["w1", "w2"], 1)
    nodes += gather_messages("o", 64, 384, 640, [], 2)

    def step(name, deps, span):
        nodes.append(Node(name, "core", deps, span, (len(nodes),)))

    step("tables", [], 1.5)
    step("place", ["rows"], 1.3)
    every = [n for dz in DZ for which in (0, 1) for n in needs("k", dz, which, WIDE_GROUPS)]
    step("kv", every + x_all + ["tables"], 1.0)
    for dz in DZ:
        step(f"Q{dz}", needs("q", dz, 0) + needs("q", dz, 1) + x_all, 0.45)
    step("rope", [f"Q{dz}" for dz in DZ] + ["tables"], 0.6)
    step("vt", ["h0", "h1", "h2", "h1s", "h2s"], 0.2)
    for qb in (0, 1):
        for pair in (0, 1):
            step(f"A{qb}{pair}", ["rope", "vt"], 0.8)
            nodes.append(Node(f"a{qb}{pair}", "peer", [f"A{qb}{pair}"], 65))
    for dz in DZ:
        for which in (0, 1):
            step(f"O{dz},{which}", needs("o", dz, which) + [f"a{qb}{pair}" for qb in (0, 1) for pair in (0, 1)], 0.3)
    return nodes


def plan():
    nodes = all_nodes()
    free, arrival, actions = {}, {}, []
    pending = list(nodes)
    while pending:
        best = None
        by_link = {}
        for m in pending:
            if all(d in arrival for d in m.deps):
                at = max([arrival[d] for d in m.deps], default=0.0)
                by_link.setdefault(m.link, []).append((at, m))
        for link, options in by_link.items():
            begin = max(free.get(link, 0.0), min(at for at, _ in options))
            at, m = min(((at, m) for at, m in options if at <= begin), key=lambda p: p[1].prio)
            if best is None or begin < best[0]:
                best = (begin, m, at)
        begin, m, at = best
        if m.link == "core":
            span, latency = m.size, 0.0
        elif m.link == "peer":
            span, latency = m.size / PEER_RATE, PEER_LATENCY
        else:
            span, latency = m.size / LINK_RATE, LINK_LATENCY
        free[m.link] = begin + span
        arrival[m.name] = begin + span + latency
        pending.remove(m)
        if m.link == "core":
            actions.append((begin, 2, "step", m.name))
        else:
            actions.append((max(at, begin - AHEAD), 1, "send", m.name))
            actions.append((arrival[m.name], 0, "recv", m.name))
    actions.sort(key=lambda a: a[:2])
    return nodes, actions, arrival


def kernel(messages, actions, tokens, table, lens, qw, kw, vw, ow, out,
           k2, q1, q2, o1, o2, tk, tb, ln, wide, rows_out, rows_in, xs, acck, acc1, acc2, cs, bias, qs, kv, vt, att, part, rs,
           lsem, send, recv, rsend, rrecv, psend, precv):
    ctx, x = lax.axis_index("ctx"), lax.axis_index("head")
    z, y, core = ctx // 8, (ctx // 2) % 4, ctx % 2
    chip = ctx // 2
    other = 1 - core
    buffers = {"k2": k2, "q1": q1, "q2": q2, "o1": o1, "o2": o2}
    number = {m.name: i for i, m in enumerate(messages)}

    def at(dz, dy, which, dx=0):
        return ((lax.rem(z + dz + 8, 8) * 4 + lax.rem(y + dy + 4, 4)) * 2 + which, lax.rem(x + dx + 4, 4))

    def chip_at(by, which):
        return (lax.rem(chip + by + 32, 32) * 2 + which, x)

    across = at(0, 0, other)
    mine = pl.ds(pl.multiple_of(core * 64, 64), 64)
    theirs = pl.ds(pl.multiple_of(other * 64, 64), 64)

    def columns(which, part):
        lo, n = ((0, 256), (256, 256))[part]
        return pl.ds(pl.multiple_of(which * 512 + lo, 128), n)

    def local(i, src, dst):
        return pltpu.make_async_copy(src, dst, lsem.at[i])

    own_kv = [local(7, kw, k2.at[0, 0, mine]), local(7, vw, k2.at[0, 0, mine])]
    early = [local(0, tokens, tk), local(1, table, tb), local(2, lens, ln)]
    late = [
        local(3, qw.at[:, columns(core, 0)], q1.at[0, 0, mine]),
        local(4, qw.at[:, columns(core, 1)], q2.at[0, 0, mine]),
        local(5, ow.at[:, pl.ds(0, 384)], o1.at[0, 0]),
        local(6, ow.at[:, pl.ds(384, 640)], o2.at[0, 0]),
    ]
    for copy in early + late:
        copy.start()
    for which in (0, 1):

        @pl.when(core == which)
        def _():
            own_kv[which].start()

    peers = [across] + [at(0, 0, which, dx) for dx in (1, 2, 3) for which in (0, 1)]
    peers += [chip_at(by, other) for by in (1, 2, -1, -2)]
    barrier = pltpu.get_barrier_semaphore()
    for peer in peers:
        pl.semaphore_signal(barrier, inc=1, device_id=peer, device_id_type=MESH)

    @pl.loop(1, 32)
    def _(by):
        pl.semaphore_signal(barrier, inc=1, device_id=chip_at(by, core), device_id_type=MESH)

    for copy in early:
        copy.wait()
    i0 = lax.broadcasted_iota(jnp.int32, (128, 128), 0)
    i1 = lax.broadcasted_iota(jnp.int32, (128, 128), 1)
    goal_row = jnp.broadcast_to((tb[pl.ds(ctx, 1), :] >> 7).astype(F32), (128, 128))
    goal_col = jnp.sum(jnp.where(i0 == i1, goal_row, 0.0), axis=1, keepdims=True)
    rank = jnp.sum(jnp.where((goal_col == goal_row) & (i0 < i1), 1.0, 0.0), axis=0, keepdims=True)
    slot = 3.0 * goal_row[:1] + rank
    pick = jnp.where(lax.broadcasted_iota(jnp.int32, (192, 128), 0).astype(F32) == slot, 1.0, 0.0).astype(BF16)
    picked = jnp.dot(pick, tk[...], preferred_element_type=F32)
    for j in range(8):
        wide[pl.ds(j, 192, stride=8), :] = picked[:, 128 * j : 128 * j + 128]
    rows_out[...] = wide[0:1536, :].astype(BF16).reshape(32, 48, 128)
    pl.semaphore_wait(barrier, len(peers) + 31)

    def row_copy(by, coming=False):
        goal, origin = lax.rem(chip + by, 32), lax.rem(chip + 32 - by, 32)
        src, dst = rows_out.at[goal], rows_in.at[chip, core]
        if coming:
            src = dst = rows_in.at[origin, core]
        return pltpu.make_async_remote_copy(
            src_ref=src, dst_ref=dst, send_sem=rsend.at[by], recv_sem=rrecv.at[by],
            device_id=chip_at(by, core), device_id_type=MESH,
        )

    @pl.loop(0, 31)
    def _(i):
        row_copy(1 + lax.rem(i + 15, 31)).start()

    keep = local(8, rows_out.at[chip], rows_in.at[chip, core])
    keep.start()
    for copy in late:
        copy.wait()
    own_kv[0].wait()

    x_low, x_high, x_far = lax.rem(x + 3, 4), lax.rem(x + 1, 4), lax.rem(x + 2, 4)
    top, bottom = pl.ds(0, 64), pl.ds(64, 64)
    far_keys, near_keys, own_keys, upper_keys = pl.ds(0, 128), pl.ds(128, 256), pl.ds(384, 256), pl.ds(512, 128)
    special = {
        "w1": (qw.at[:, columns(other, 0)], q1.at[0, 0, mine], q1.at[0, 0, theirs], across),
        "w2": (qw.at[:, columns(other, 1)], q2.at[0, 0, mine], q2.at[0, 0, theirs], across),
        "rows": (rows_in.at[:, core], rows_in.at[:, core], rows_in.at[:, other], across),
        "x+a": (xs.at[x, core, top], xs.at[x, core, top], xs.at[x_low, core, top], at(0, 0, core, 1)),
        "x+b": (xs.at[x, core, bottom], xs.at[x, core, bottom], xs.at[x_low, core, bottom], at(0, 0, core, 1)),
        "x-a": (xs.at[x, core, top], xs.at[x, core, top], xs.at[x_high, core, top], at(0, 0, core, -1)),
        "x-b": (xs.at[x, core, bottom], xs.at[x, core, bottom], xs.at[x_high, core, bottom], at(0, 0, core, -1)),
        "x+2": (xs.at[x_low, core, top], xs.at[x_low, core, top], xs.at[x_far, core, top], at(0, 0, core, 1)),
        "x-2": (xs.at[x_high, core, bottom], xs.at[x_high, core, bottom], xs.at[x_far, core, bottom],
                at(0, 0, core, -1)),
        "xs+": (xs.at[x_low, core], xs.at[x_low, core], xs.at[x_low, other], across),
        "xs-": (xs.at[x_high, core], xs.at[x_high, core], xs.at[x_high, other], across),
        "xs2": (xs.at[x_far, core], xs.at[x_far, core], xs.at[x_far, other], across),
        "h0": (kv.at[core, own_keys], kv.at[core, own_keys], kv.at[other, own_keys], across),
        "h1": (kv.at[core, own_keys], kv.at[core, near_keys], kv.at[core, near_keys], chip_at(1, core)),
        "h2": (kv.at[core, upper_keys], kv.at[core, far_keys], kv.at[core, far_keys], chip_at(2, core)),
        "h1s": (kv.at[core, near_keys], kv.at[core, near_keys], kv.at[other, near_keys], across),
        "h2s": (kv.at[core, far_keys], kv.at[core, far_keys], kv.at[other, far_keys], across),
    }
    for qb in (0, 1):
        for pair in (0, 1):
            special[f"a{qb}{pair}"] = (att.at[core, pair, qb], att.at[core, pair, qb], att.at[other, pair, qb], across)
    to = {"+z": at(1, 0, core), "-z": at(-1, 0, core), "+y": at(0, 1, core), "-y": at(0, -1, core)}

    def view(place):
        name, a, b, (lo, n) = place
        b = pl.ds(*b) if isinstance(b, tuple) else b
        return buffers[name].at[a, b, pl.ds(lo, n)]

    def remote(src, dst, ssem, rsem, device):
        return pltpu.make_async_remote_copy(
            src_ref=src, dst_ref=dst, send_sem=ssem, recv_sem=rsem, device_id=device, device_id_type=MESH
        )

    def copy_of(m, coming=False):
        i = number[m.name]
        if m.name in special:
            src, dst, land, device = special[m.name]
        else:
            src, dst, land, device = view(m.src), view(m.dst), view(m.dst), to[m.link]
        if coming:
            src = dst = land
        return remote(src, dst, send.at[i], recv.at[i], device)

    by_name = {m.name: m for m in messages}

    def kv_copy(which):
        i = number["w3"]
        src = (vw, kw)[which]
        return remote(src, k2.at[0, 0, mine], send.at[i], recv.at[i], across)

    def place():
        t = tb[...]
        upper = jnp.where(i0 < i1, 1.0, 0.0).astype(BF16)
        landing = []
        for half in (0, 1):
            here = (t >> 7) == 2 * chip + half
            nth = jnp.dot(jnp.where(here, 1.0, 0.0).astype(BF16), upper, preferred_element_type=F32)
            row = ((t & 255) + 1).astype(F32)
            for k in range(3):
                landing.append(jnp.sum(jnp.where(here & (nth == float(k)), row, 0.0), axis=1, keepdims=True))
        goal = jnp.concatenate(landing, axis=0)
        lane = lax.broadcasted_iota(jnp.int32, (384, 256), 1).astype(F32) + 1.0
        spot = jnp.transpose(jnp.where(goal == lane, 1.0, 0.0)).astype(BF16)
        wide[...] = rows_in[...].astype(F32).reshape(3072, 128)
        for j in range(8):
            rows = [wide[pl.ds(8 * n + j, 64, stride=48), :] for n in range(6)]
            rows = jnp.concatenate(rows, axis=0).astype(BF16)
            found = jnp.dot(spot, rows, preferred_element_type=F32).astype(BF16)
            xs[x, :, :, 128 * j : 128 * j + 128] = found.reshape(2, 128, 128)

    pseudo = ("r+z", "r-z", "r+y", "r-y")

    def start_message(name):
        if name == "rows":
            keep.wait()

            @pl.loop(1, 32)
            def _(by):
                row_copy(by, True).wait_recv()

        if name == "w3":
            for which in (0, 1):

                @pl.when(core == which)
                def _():
                    kv_copy(which).start()

        elif name not in pseudo:
            copy_of(by_name[name]).start()

    def finish_message(name):
        if name == "w3":
            i = number["w3"]
            land = k2.at[0, 0, theirs]
            remote(land, land, send.at[i], recv.at[i], across).wait_recv()
        elif name not in pseudo:
            copy_of(by_name[name], True).wait_recv()

    def tables():
        base = chip * 256
        d0 = lax.broadcasted_iota(jnp.int32, (64, 64), 0)
        d1 = lax.broadcasted_iota(jnp.int32, (64, 64), 1)
        spread = jnp.broadcast_to(ln[...].astype(F32), (64, 64))
        end_col = jnp.sum(jnp.where(d1 <= d0, spread, 0.0), axis=1, keepdims=True)
        len_col = jnp.sum(jnp.where(d1 == d0, spread, 0.0), axis=1, keepdims=True)
        end_row = jnp.sum(jnp.where(d0 <= d1, jnp.broadcast_to(len_col, (64, 64)), 0.0), axis=0, keepdims=True)
        row_id = (base + lax.broadcasted_iota(jnp.int32, (64, 256), 1)).astype(F32)
        before = row_id >= end_col
        q_doc = jnp.sum(jnp.where(before, 1.0, 0.0), axis=0, keepdims=True)
        position = row_id - jnp.sum(jnp.where(before, len_col, 0.0), axis=0, keepdims=True)
        turn = lax.broadcasted_iota(jnp.int32, (64, 256), 0).astype(F32)
        angle = position * jnp.exp(turn * (-2.0 / HD * math.log(ROPE_BASE)))
        cs[...] = jnp.transpose(jnp.concatenate([jnp.cos(angle), jnp.sin(angle)], axis=0))
        key_id = base - 384 + lax.broadcasted_iota(jnp.int32, (640, 64), 0)
        k_doc = jnp.sum(jnp.where(key_id.astype(F32) >= end_row, 1.0, 0.0), axis=1, keepdims=True)
        for qb in (0, 1):
            lo = 128 * qb
            kid = base - 384 + lo + lax.broadcasted_iota(jnp.int32, (512, 128), 0)
            qid = base + lo + lax.broadcasted_iota(jnp.int32, (512, 128), 1)
            allowed = (k_doc[lo : lo + 512] == q_doc[:, lo : lo + 128]) & (kid <= qid) & (kid >= 0)
            bias[qb] = jnp.where(allowed, 0.0, -jnp.inf)

    def columns_of(dz):
        zz = lax.rem(z + dz + 8, 8)
        parts = []
        for dy in DY:
            lane = pl.multiple_of((lax.rem(zz, 2) * 4 + lax.rem(y + dy + 4, 4)) * 128, 128)
            parts.append(xs[zz // 2, :, :, pl.ds(lane, 128)].reshape(256, 128))
        return jnp.concatenate(parts, axis=1)

    def project(dz):
        s = ZS[dz]
        lhs = columns_of(dz)
        one = jnp.dot(lhs, q1[s].reshape(512, 256), preferred_element_type=F32)
        two = jnp.dot(lhs, q2[:, s].reshape(512, 256), preferred_element_type=F32)
        if dz == 0:
            acc1[...] = one
            acc2[...] = two
        else:
            acc1[...] += one
            acc2[...] += two

    def turned_pairs():
        table = cs[...]
        swapped = pltpu.roll(table, 64, 1)
        low = lax.broadcasted_iota(jnp.int32, (256, 128), 1) < 64
        return jnp.where(low, table, swapped), jnp.where(low, -swapped, table)

    def rope(e):
        cosine, sine = turned_pairs()
        return e * cosine + pltpu.roll(e, 64, 1) * sine

    def make_kv():
        raw = None
        for dz in DZ:
            term = jnp.dot(columns_of(dz), k2[:, ZS[dz]].reshape(512, 128), preferred_element_type=F32)
            raw = term if raw is None else raw + term
        acck[...] = raw
        raw = acck[...]
        kv[core, 384:640] = jnp.where(core == 0, rope(raw), raw).astype(BF16)

    def rope_queries():
        for h in range(4):
            e = acc1[:, 128 * h : 128 * h + 128] if h < 2 else acc2[:, 128 * (h - 2) : 128 * (h - 2) + 128]
            turned_e = rope(e).astype(BF16)
            for qb in (0, 1):
                qs[qb, h // 2, 128 * (h % 2) : 128 * (h % 2) + 128] = turned_e[128 * qb : 128 * qb + 128]

    def turn_values():
        eye = (
            lax.broadcasted_iota(jnp.int32, (128, 128), 0) == lax.broadcasted_iota(jnp.int32, (128, 128), 1)
        ).astype(F32).astype(BF16)
        vt[...] = lax.dot_general(eye, kv[1], (((1,), (1,)), ((), ())), preferred_element_type=F32).astype(BF16)

    def attend(qb, pair):
        keys = kv[0, 128 * qb : 128 * qb + 512]
        scores = lax.dot_general(keys, qs[qb, pair], (((1,), (1,)), ((), ())), preferred_element_type=F32)
        mask = bias[qb]
        scores = scores * (1.0 / math.sqrt(HD)) + jnp.concatenate([mask, mask], axis=1)
        expo = jnp.exp(scores - jnp.max(scores, axis=0, keepdims=True))
        denominator = jnp.sum(expo, axis=0, keepdims=True)
        summed = jnp.dot(vt[:, 128 * qb : 128 * qb + 512], expo.astype(BF16), preferred_element_type=F32)
        result = (summed / denominator).astype(BF16)
        for h in (0, 1):
            att[core, pair, qb, 128 * h : 128 * h + 128] = result[:, 128 * h : 128 * h + 128]

    def part_copy(dz, which, t, start):
        s = ZS[dz]
        zz = lax.rem(z + dz + 8, 8)
        goal = zz // 2
        here = (goal == x) & (core == t)
        sem = precv.at[core, x, lax.rem(zz, 2), which]
        land = rs.at[core, x, lax.rem(zz, 2), which]

        @pl.when(jnp.logical_not(here))
        def _():
            copy = remote(part.at[s, which, t], land, psend.at[s, which, t], sem, (chip * 2 + t, goal))
            copy.start() if start else copy.wait_send()

        if start:

            @pl.when(here)
            def _():
                pltpu.make_async_copy(part.at[s, which, t], land, sem).start()

    def out_project(dz, which):
        s = ZS[dz]
        dy = slice(2 * which, 2 * which + 2)
        weights = jnp.concatenate([att[:, :, 0].reshape(1024, 128), att[:, :, 1].reshape(1024, 128)], axis=1)
        total = jnp.dot(o1[s, dy].reshape(128, 384), weights[:384], preferred_element_type=F32)
        total += jnp.dot(o2[dy, s].reshape(128, 640), weights[384:], preferred_element_type=F32)
        total = total.astype(BF16)
        for t in (0, 1):
            part[s, which, t] = total[:, 128 * t : 128 * t + 128]
            part_copy(dz, which, t, True)

    def run(name):
        if name == "tables":
            tables()
        elif name == "place":
            place()
        elif name == "kv":
            make_kv()
        elif name == "rope":
            rope_queries()
        elif name == "vt":
            turn_values()
        elif name[0] == "A":
            attend(int(name[1]), int(name[2]))
        elif name[0] == "Q":
            project(int(name[1:]))
        else:
            dz, which = name[1:].split(",")
            out_project(int(dz), int(which))

    for _, _, kind, name in actions:
        if kind == "send":
            start_message(name)
        elif kind == "recv":
            finish_message(name)
        else:
            run(name)

    @pl.loop(1, 32)
    def _(by):
        row_copy(by).wait_send()

    kv_copy(0).wait_send()
    for m in messages:
        if m.name not in pseudo and m.name != "w3":
            copy_of(m).wait_send()
    for dz in DZ:
        for which in (0, 1):
            for t in (0, 1):
                part_copy(dz, which, t, False)
    for zz in (0, 1):
        sums = []
        for c in (0, 1):
            total = None
            for g in range(4):
                for which in (0, 1):
                    land = rs.at[c, g, zz, which]
                    remote(land, land, psend.at[0, 0, 0], precv.at[c, g, zz, which], across).wait_recv()
                term = rs[c, g, zz].reshape(256, 128).astype(F32)
                total = term if total is None else total + term
            sums.append(total)
        for dy in DY:
            s = YS[dy]
            block = jnp.concatenate([sums[0][64 * s : 64 * s + 64], sums[1][64 * s : 64 * s + 64]], axis=0)
            lane = pl.multiple_of((zz * 4 + lax.rem(y + dy + 4, 4)) * 128, 128)
            out[:, pl.ds(lane, 128)] = jnp.transpose(block).astype(BF16)


def per_device(tokens, context_row, lengths, qw, kw, vw, ow):
    nodes, actions, _ = plan()
    messages = [n for n in nodes if n.link != "core"]
    count = len(messages)
    dma = pltpu.SemaphoreType.DMA
    scratch = [
        pltpu.VMEM((4, 8, 128, 128), BF16),
        pltpu.VMEM((8, 4, 128, 256), BF16),
        pltpu.VMEM((4, 8, 128, 256), BF16),
        pltpu.VMEM((8, 4, 64, 384), BF16),
        pltpu.VMEM((4, 8, 64, 640), BF16),
        pltpu.VMEM((128, 1024), BF16),
        pltpu.VMEM((64, 128), jnp.int32),
        pltpu.VMEM((1, 64), jnp.int32),
        pltpu.VMEM((3072, 128), F32),
        pltpu.VMEM((32, 48, 128), BF16),
        pltpu.VMEM((32, 2, 48, 128), BF16),
        pltpu.VMEM((4, 2, 128, 1024), BF16),
        pltpu.VMEM((256, 128), F32),
        pltpu.VMEM((256, 256), F32),
        pltpu.VMEM((256, 256), F32),
        pltpu.VMEM((256, 128), F32),
        pltpu.VMEM((2, 512, 128), F32),
        pltpu.VMEM((2, 2, 256, 128), BF16),
        pltpu.VMEM((2, 640, 128), BF16),
        pltpu.VMEM((128, 640), BF16),
        pltpu.VMEM((2, 2, 2, 256, 128), BF16),
        pltpu.VMEM((8, 2, 2, 128, 128), BF16),
        pltpu.VMEM((2, 4, 2, 2, 128, 128), BF16),
        dma((9,)),
        dma((count,)),
        dma((count,)),
        dma((32,)),
        dma((32,)),
        dma((8, 2, 2)),
        dma((2, 4, 2, 2)),
    ]

    def body(*refs):
        kernel(messages, actions, *refs)

    return pl.pallas_call(
        body,
        out_shape=jax.ShapeDtypeStruct((128, 1024), BF16),
        in_specs=[pl.BlockSpec(memory_space=pltpu.HBM)] * 7,
        out_specs=pl.BlockSpec(memory_space=pltpu.VMEM),
        scratch_shapes=scratch,
        compiler_params=pltpu.CompilerParams(
            collective_id=0, has_side_effects=True, vmem_limit_bytes=63 * 2**20
        ),
    )(tokens, context_row.reshape(64, 128), lengths.reshape(1, 64), qw, kw, vw, ow.T)


def solution(mesh):
    return jax.shard_map(
        per_device,
        mesh=mesh,
        in_specs=(
            P("ctx", "head"),
            P(),
            P(),
            P("ctx", "head"),
            P("ctx", "head"),
            P("ctx", "head"),
            P("head", "ctx"),
        ),
        out_specs=P("ctx", "head"),
        check_vma=False,
    )
```

```python
import math

import jax
import jax.numpy as jnp
from jax import lax
from jax.experimental import pallas as pl
from jax.experimental.pallas import tpu as pltpu
from jax.sharding import PartitionSpec as P

MESH = pl.DeviceIdType.MESH
F32 = jnp.float32
BF16 = jnp.bfloat16
ROPE_BASE = 500000.0
HD = 128

DZ = (0, 1, -1, 2, -2, 3, -3, 4)
DY = (0, 1, -1, 2)
ZS = {d: i for i, d in enumerate(DZ)}
YS = {d: i for i, d in enumerate(DY)}
GROUPS = ((0, 1), (1, 3), (3, 5), (5, 7), (7, 8))
WIDE_GROUPS = ((0, 3), (3, 7), (7, 8))

LINK_RATE, LINK_LATENCY = 44, 3.2
PEER_RATE, PEER_LATENCY = 400.0, 1.0
AHEAD = 1.0
EXTRA = {"r": 4.0, "x": 1.0, "h": 1.0, "a": 0.5}


class Node:
    def __init__(self, name, link, deps, size, prio=(0,), src=None, dst=None):
        self.name, self.link, self.deps, self.size, self.prio = name, link, deps, size, prio
        self.src, self.dst = src, dst


def gather_messages(tag, rows, width1, width2, ready, rank, groups=GROUPS):
    out = []
    half = rows // 2
    size1 = rows * width1 * 2e-3
    size2 = rows * width2 * 2e-3
    full, top, bottom = (0, rows), (0, half), (half, half)

    def one(dz, dy, part):
        return (tag + "1", ZS[dz], YS[dy], part)

    def pair(dz, which):
        return (tag + "1", ZS[dz], (2 * which, 2), full)

    def two(dy, dz, part):
        return (tag + "2", YS[dy], ZS[dz], part)

    def group(dy, g):
        lo, hi = groups[g]
        return (tag + "2", YS[dy], (lo, hi - lo), full)

    def add(name, link, src, dst, deps, size, prio):
        out.append(Node(tag + name, link, [tag + d for d in deps] + ready, size, (rank,) + prio, src, dst))

    if width1:
        add("1y+1", "+y", one(0, 0, full), one(0, -1, full), [], size1, (0, 1))
        add("1y-1", "-y", one(0, 0, full), one(0, 1, full), [], size1, (0, 1))
        add("1y+2", "+y", one(0, -1, top), one(0, 2, top), ["1y+1"], size1 / 2, (0, 2))
        add("1y-2", "-y", one(0, 1, bottom), one(0, 2, bottom), ["1y-1"], size1 / 2, (0, 2))
    first = {0: ["1y-1"], 1: ["1y+1", "1y+2", "1y-2"]}
    for which in (0, 1) if width1 else ():
        for sign, link in ((1, "+z"), (-1, "-z")):
            mark = "+" if sign > 0 else "-"
            for step in (1, 2, 3, 4):
                if step == 4 and (sign > 0) != (which == 0):
                    continue
                deps = first[which] if step == 1 else [f"1z{which}{mark}{step - 1}"]
                far = 4 if step == 4 else -sign * step
                add(f"1z{which}{mark}{step}", link, pair(-sign * (step - 1), which), pair(far, which), deps,
                    2 * size1, (1, step))
    for sign, link in ((1, "+z"), (-1, "-z")):
        mark = "+" if sign > 0 else "-"
        for step in (1, 2, 3, 4):
            deps = [] if step == 1 else [f"2z{mark}{step - 1}"]
            part = full if step < 4 else (top if sign > 0 else bottom)
            far = 4 if step == 4 else -sign * step
            add(f"2z{mark}{step}", link, two(0, -sign * (step - 1), part), two(0, far, part), deps,
                size2 if step < 4 else size2 / 2, (0, step))
    for g, (lo, hi) in enumerate(groups):
        deps = []
        for dz in DZ[lo:hi]:
            deps += z_messages(dz)
        amount = size2 * (hi - lo)
        add(f"2y{g}+1", "+y", group(0, g), group(-1, g), deps, amount, (1, g))
        add(f"2y{g}-1", "-y", group(0, g), group(1, g), deps, amount, (1, g))
        if g % 2 == 0:
            add(f"2y{g}+2", "+y", group(-1, g), group(2, g), [f"2y{g}+1"], amount, (1, g))
        else:
            add(f"2y{g}-2", "-y", group(1, g), group(2, g), [f"2y{g}-1"], amount, (1, g))
    return out


def z_messages(dz):
    if dz == 0:
        return []
    return ["2z+4", "2z-4"] if dz == 4 else [f"2z{'+' if dz < 0 else '-'}{abs(dz)}"]


def needs(tag, dz, which, groups=GROUPS):
    g = [i for i, (lo, hi) in enumerate(groups) if lo <= ZS[dz] < hi][0]
    if which == 0:
        names = z_messages(dz) + [f"2y{g}-1"]
    else:
        names = [f"2y{g}+1", f"2y{g}+2" if g % 2 == 0 else f"2y{g}-2"]
    if tag != "k":
        if dz == 0:
            names += ["1y-1"] if which == 0 else ["1y+1", "1y+2", "1y-2"]
        elif dz == 4:
            names += ["1z0+4"] if which == 0 else ["1z1-4"]
        else:
            names += [f"1z{which}{'+' if dz < 0 else '-'}{abs(dz)}"]
    return [tag + n for n in names]


def all_nodes():
    x_all = ["x+a", "x+b", "x-a", "x-b", "xs+", "xs-", "xs2"]
    nodes = [
        Node("w1", "peer", [], 33),
        Node("w2", "peer", [], 33),
        Node("w3", "peer", [], 17),
        Node("r+z", "+z", [], 384, (-2,)),
        Node("r-z", "-z", [], 384, (-2,)),
        Node("r+y", "+y", [], 192, (-2,)),
        Node("r-y", "-y", [], 192, (-2,)),
        Node("rows", "peer", ["r+z", "r-z", "r+y", "r-y"], 384, (-1,)),
        Node("x+a", "+x", ["place"], 131, (0, 0)),
        Node("x+b", "+x", ["place"], 131, (0, 1)),
        Node("x-b", "-x", ["place"], 131, (0, 0)),
        Node("x-a", "-x", ["place"], 131, (0, 1)),
        Node("x+2", "+x", ["x+a"], 131, (0, 2)),
        Node("x-2", "-x", ["x-b"], 131, (0, 2)),
        Node("xs+", "peer", ["x+a", "x+b"], 262, (1,)),
        Node("xs-", "peer", ["x-a", "x-b"], 262, (1,)),
        Node("xs2", "peer", ["x+2", "x-2"], 262, (1,)),
        Node("h0", "peer", ["kv"], 65, (0,)),
        Node("h1", "+y", ["kv"], 85, (-1, 0)),
        Node("h2", "+y", ["kv"], 65, (-1, 1)),
        Node("h1s", "peer", ["h1"], 65, (0,)),
        Node("h2s", "peer", ["h2"], 33, (0,)),
    ]
    nodes += gather_messages("k", 128, 0, 128, ["w3"], 0, WIDE_GROUPS)
    nodes += gather_messages("q", 128, 256, 256, ["w1", "w2"], 1)
    nodes += gather_messages("o", 64, 384, 640, [], 2)

    def step(name, deps, span):
        nodes.append(Node(name, "core", deps, span, (len(nodes),)))

    step("tables", [], 1.5)
    step("place", ["rows"], 1.3)
    every = [n for dz in DZ for which in (0, 1) for n in needs("k", dz, which, WIDE_GROUPS)]
    step("kv", every + x_all + ["tables"], 1.0)
    for dz in DZ:
        step(f"Q{dz}", needs("q", dz, 0) + needs("q", dz, 1) + x_all, 0.45)
    step("rope", [f"Q{dz}" for dz in DZ] + ["tables"], 0.6)
    step("vt", ["h0", "h1", "h2", "h1s", "h2s"], 0.2)
    for qb in (0, 1):
        for pair in (0, 1):
            step(f"A{qb}{pair}", ["rope", "vt"], 0.8)
            nodes.append(Node(f"a{qb}{pair}", "peer", [f"A{qb}{pair}"], 65))
    for dz in DZ:
        for which in (0, 1):
            step(f"O{dz},{which}", needs("o", dz, which) + [f"a{qb}{pair}" for qb in (0, 1) for pair in (0, 1)], 0.3)
    return nodes


def plan():
    nodes = all_nodes()
    free, arrival, actions = {}, {}, []
    pending = list(nodes)
    while pending:
        best = None
        by_link = {}
        for m in pending:
            if all(d in arrival for d in m.deps):
                at = max([arrival[d] for d in m.deps], default=0.0)
                by_link.setdefault(m.link, []).append((at, m))
        for link, options in by_link.items():
            begin = max(free.get(link, 0.0), min(at for at, _ in options))
            at, m = min(((at, m) for at, m in options if at <= begin), key=lambda p: p[1].prio)
            if best is None or begin < best[0]:
                best = (begin, m, at)
        begin, m, at = best
        if m.link == "core":
            span, latency = m.size, 0.0
        elif m.link == "peer":
            span, latency = m.size / PEER_RATE, PEER_LATENCY
        else:
            span, latency = m.size / LINK_RATE, LINK_LATENCY
        latency += EXTRA.get(m.name[0], 0.0) if m.link != "core" and m.name != "rows" else 0.0
        free[m.link] = begin + span
        arrival[m.name] = begin + span + latency
        pending.remove(m)
        if m.link == "core":
            actions.append((begin, 2, "step", m.name))
        else:
            actions.append((max(at, begin - AHEAD), 1, "send", m.name))
            actions.append((arrival[m.name], 0, "recv", m.name))
    actions.sort(key=lambda a: a[:2])
    return nodes, actions, arrival


def kernel(messages, actions, tokens, table, lens, qw, kw, vw, ow, out,
           k2, q1, q2, o1, o2, tk, tb, ln, wide, rows_out, rows_in, xs, acck, acc1, acc2, cs, bias, qs, kv, vt, att, part, rs,
           lsem, send, recv, rsend, rrecv, psend, precv):
    ctx, x = lax.axis_index("ctx"), lax.axis_index("head")
    z, y, core = ctx // 8, (ctx // 2) % 4, ctx % 2
    chip = ctx // 2
    other = 1 - core
    buffers = {"k2": k2, "q1": q1, "q2": q2, "o1": o1, "o2": o2}
    number = {m.name: i for i, m in enumerate(messages)}

    def at(dz, dy, which, dx=0):
        return ((lax.rem(z + dz + 8, 8) * 4 + lax.rem(y + dy + 4, 4)) * 2 + which, lax.rem(x + dx + 4, 4))

    def chip_at(by, which):
        return (lax.rem(chip + by + 32, 32) * 2 + which, x)

    across = at(0, 0, other)
    mine = pl.ds(pl.multiple_of(core * 64, 64), 64)
    theirs = pl.ds(pl.multiple_of(other * 64, 64), 64)

    def columns(which, part):
        lo, n = ((0, 256), (256, 256))[part]
        return pl.ds(pl.multiple_of(which * 512 + lo, 128), n)

    def local(i, src, dst):
        return pltpu.make_async_copy(src, dst, lsem.at[i])

    own_kv = [local(7, kw, k2.at[0, 0, mine]), local(7, vw, k2.at[0, 0, mine])]
    early = [local(0, tokens, tk), local(1, table, tb), local(2, lens, ln)]
    late = [
        local(3, qw.at[:, columns(core, 0)], q1.at[0, 0, mine]),
        local(4, qw.at[:, columns(core, 1)], q2.at[0, 0, mine]),
        local(5, ow.at[:, pl.ds(0, 384)], o1.at[0, 0]),
        local(6, ow.at[:, pl.ds(384, 640)], o2.at[0, 0]),
    ]
    for copy in early + late:
        copy.start()
    for which in (0, 1):

        @pl.when(core == which)
        def _():
            own_kv[which].start()

    peers = [across] + [at(0, 0, which, dx) for dx in (1, 2, 3) for which in (0, 1)]
    peers += [chip_at(by, other) for by in (1, 2, -1, -2)]
    barrier = pltpu.get_barrier_semaphore()
    for peer in peers:
        pl.semaphore_signal(barrier, inc=1, device_id=peer, device_id_type=MESH)

    @pl.loop(1, 32)
    def _(by):
        pl.semaphore_signal(barrier, inc=1, device_id=chip_at(by, core), device_id_type=MESH)

    for copy in early:
        copy.wait()
    i0 = lax.broadcasted_iota(jnp.int32, (128, 128), 0)
    i1 = lax.broadcasted_iota(jnp.int32, (128, 128), 1)
    goal_row = jnp.broadcast_to((tb[pl.ds(ctx, 1), :] >> 7).astype(F32), (128, 128))
    goal_col = jnp.sum(jnp.where(i0 == i1, goal_row, 0.0), axis=1, keepdims=True)
    rank = jnp.sum(jnp.where((goal_col == goal_row) & (i0 < i1), 1.0, 0.0), axis=0, keepdims=True)
    slot = 3.0 * goal_row[:1] + rank
    pick = jnp.where(lax.broadcasted_iota(jnp.int32, (192, 128), 0).astype(F32) == slot, 1.0, 0.0).astype(BF16)
    picked = jnp.dot(pick, tk[...], preferred_element_type=F32)
    for j in range(8):
        wide[pl.ds(j, 192, stride=8), :] = picked[:, 128 * j : 128 * j + 128]
    rows_out[...] = wide[0:1536, :].astype(BF16).reshape(32, 48, 128)
    pl.semaphore_wait(barrier, len(peers) + 31)

    def row_copy(by, coming=False):
        goal, origin = lax.rem(chip + by, 32), lax.rem(chip + 32 - by, 32)
        src, dst = rows_out.at[goal], rows_in.at[chip, core]
        if coming:
            src = dst = rows_in.at[origin, core]
        return pltpu.make_async_remote_copy(
            src_ref=src, dst_ref=dst, send_sem=rsend.at[by], recv_sem=rrecv.at[by],
            device_id=chip_at(by, core), device_id_type=MESH,
        )

    @pl.loop(0, 31)
    def _(i):
        row_copy(1 + lax.rem(i + 15, 31)).start()

    keep = local(8, rows_out.at[chip], rows_in.at[chip, core])
    keep.start()
    for copy in late:
        copy.wait()
    own_kv[0].wait()

    x_low, x_high, x_far = lax.rem(x + 3, 4), lax.rem(x + 1, 4), lax.rem(x + 2, 4)
    top, bottom = pl.ds(0, 64), pl.ds(64, 64)
    far_keys, near_keys, own_keys, upper_keys = pl.ds(0, 128), pl.ds(128, 256), pl.ds(384, 256), pl.ds(512, 128)
    special = {
        "w1": (qw.at[:, columns(other, 0)], q1.at[0, 0, mine], q1.at[0, 0, theirs], across),
        "w2": (qw.at[:, columns(other, 1)], q2.at[0, 0, mine], q2.at[0, 0, theirs], across),
        "rows": (rows_in.at[:, core], rows_in.at[:, core], rows_in.at[:, other], across),
        "x+a": (xs.at[x, core, top], xs.at[x, core, top], xs.at[x_low, core, top], at(0, 0, core, 1)),
        "x+b": (xs.at[x, core, bottom], xs.at[x, core, bottom], xs.at[x_low, core, bottom], at(0, 0, core, 1)),
        "x-a": (xs.at[x, core, top], xs.at[x, core, top], xs.at[x_high, core, top], at(0, 0, core, -1)),
        "x-b": (xs.at[x, core, bottom], xs.at[x, core, bottom], xs.at[x_high, core, bottom], at(0, 0, core, -1)),
        "x+2": (xs.at[x_low, core, top], xs.at[x_low, core, top], xs.at[x_far, core, top], at(0, 0, core, 1)),
        "x-2": (xs.at[x_high, core, bottom], xs.at[x_high, core, bottom], xs.at[x_far, core, bottom],
                at(0, 0, core, -1)),
        "xs+": (xs.at[x_low, core], xs.at[x_low, core], xs.at[x_low, other], across),
        "xs-": (xs.at[x_high, core], xs.at[x_high, core], xs.at[x_high, other], across),
        "xs2": (xs.at[x_far, core], xs.at[x_far, core], xs.at[x_far, other], across),
        "h0": (kv.at[core, own_keys], kv.at[core, own_keys], kv.at[other, own_keys], across),
        "h1": (kv.at[core, own_keys], kv.at[core, near_keys], kv.at[core, near_keys], chip_at(1, core)),
        "h2": (kv.at[core, upper_keys], kv.at[core, far_keys], kv.at[core, far_keys], chip_at(2, core)),
        "h1s": (kv.at[core, near_keys], kv.at[core, near_keys], kv.at[other, near_keys], across),
        "h2s": (kv.at[core, far_keys], kv.at[core, far_keys], kv.at[other, far_keys], across),
    }
    for qb in (0, 1):
        for pair in (0, 1):
            special[f"a{qb}{pair}"] = (att.at[core, pair, qb], att.at[core, pair, qb], att.at[other, pair, qb], across)
    to = {"+z": at(1, 0, core), "-z": at(-1, 0, core), "+y": at(0, 1, core), "-y": at(0, -1, core)}

    def view(place):
        name, a, b, (lo, n) = place
        b = pl.ds(*b) if isinstance(b, tuple) else b
        return buffers[name].at[a, b, pl.ds(lo, n)]

    def remote(src, dst, ssem, rsem, device):
        return pltpu.make_async_remote_copy(
            src_ref=src, dst_ref=dst, send_sem=ssem, recv_sem=rsem, device_id=device, device_id_type=MESH
        )

    def copy_of(m, coming=False):
        i = number[m.name]
        if m.name in special:
            src, dst, land, device = special[m.name]
        else:
            src, dst, land, device = view(m.src), view(m.dst), view(m.dst), to[m.link]
        if coming:
            src = dst = land
        return remote(src, dst, send.at[i], recv.at[i], device)

    by_name = {m.name: m for m in messages}

    def kv_copy(which):
        i = number["w3"]
        src = (vw, kw)[which]
        return remote(src, k2.at[0, 0, mine], send.at[i], recv.at[i], across)

    def place():
        t = tb[...]
        upper = jnp.where(i0 < i1, 1.0, 0.0).astype(BF16)
        landing = []
        for half in (0, 1):
            here = (t >> 7) == 2 * chip + half
            nth = jnp.dot(jnp.where(here, 1.0, 0.0).astype(BF16), upper, preferred_element_type=F32)
            row = ((t & 255) + 1).astype(F32)
            for k in range(3):
                landing.append(jnp.sum(jnp.where(here & (nth == float(k)), row, 0.0), axis=1, keepdims=True))
        goal = jnp.concatenate(landing, axis=0)
        lane = lax.broadcasted_iota(jnp.int32, (384, 256), 1).astype(F32) + 1.0
        spot = jnp.transpose(jnp.where(goal == lane, 1.0, 0.0)).astype(BF16)
        wide[...] = rows_in[...].astype(F32).reshape(3072, 128)
        for j in range(8):
            rows = [wide[pl.ds(8 * n + j, 64, stride=48), :] for n in range(6)]
            rows = jnp.concatenate(rows, axis=0).astype(BF16)
            found = jnp.dot(spot, rows, preferred_element_type=F32).astype(BF16)
            xs[x, :, :, 128 * j : 128 * j + 128] = found.reshape(2, 128, 128)

    pseudo = ("r+z", "r-z", "r+y", "r-y")

    def start_message(name):
        if name == "rows":
            keep.wait()

            @pl.loop(1, 32)
            def _(by):
                row_copy(by, True).wait_recv()

        if name == "w3":
            for which in (0, 1):

                @pl.when(core == which)
                def _():
                    kv_copy(which).start()

        elif name not in pseudo:
            copy_of(by_name[name]).start()

    def finish_message(name):
        if name == "w3":
            i = number["w3"]
            land = k2.at[0, 0, theirs]
            remote(land, land, send.at[i], recv.at[i], across).wait_recv()
        elif name not in pseudo:
            copy_of(by_name[name], True).wait_recv()

    def tables():
        base = chip * 256
        d0 = lax.broadcasted_iota(jnp.int32, (64, 64), 0)
        d1 = lax.broadcasted_iota(jnp.int32, (64, 64), 1)
        spread = jnp.broadcast_to(ln[...].astype(F32), (64, 64))
        end_col = jnp.sum(jnp.where(d1 <= d0, spread, 0.0), axis=1, keepdims=True)
        len_col = jnp.sum(jnp.where(d1 == d0, spread, 0.0), axis=1, keepdims=True)
        end_row = jnp.sum(jnp.where(d0 <= d1, jnp.broadcast_to(len_col, (64, 64)), 0.0), axis=0, keepdims=True)
        row_id = (base + lax.broadcasted_iota(jnp.int32, (64, 256), 1)).astype(F32)
        before = row_id >= end_col
        q_doc = jnp.sum(jnp.where(before, 1.0, 0.0), axis=0, keepdims=True)
        position = row_id - jnp.sum(jnp.where(before, len_col, 0.0), axis=0, keepdims=True)
        turn = lax.broadcasted_iota(jnp.int32, (64, 256), 0).astype(F32)
        angle = position * jnp.exp(turn * (-2.0 / HD * math.log(ROPE_BASE)))
        cs[...] = jnp.transpose(jnp.concatenate([jnp.cos(angle), jnp.sin(angle)], axis=0))
        key_id = base - 384 + lax.broadcasted_iota(jnp.int32, (640, 64), 0)
        k_doc = jnp.sum(jnp.where(key_id.astype(F32) >= end_row, 1.0, 0.0), axis=1, keepdims=True)
        for qb in (0, 1):
            lo = 128 * qb
            kid = base - 384 + lo + lax.broadcasted_iota(jnp.int32, (512, 128), 0)
            qid = base + lo + lax.broadcasted_iota(jnp.int32, (512, 128), 1)
            allowed = (k_doc[lo : lo + 512] == q_doc[:, lo : lo + 128]) & (kid <= qid) & (kid >= 0)
            bias[qb] = jnp.where(allowed, 0.0, -jnp.inf)

    def columns_of(dz):
        zz = lax.rem(z + dz + 8, 8)
        parts = []
        for dy in DY:
            lane = pl.multiple_of((lax.rem(zz, 2) * 4 + lax.rem(y + dy + 4, 4)) * 128, 128)
            parts.append(xs[zz // 2, :, :, pl.ds(lane, 128)].reshape(256, 128))
        return jnp.concatenate(parts, axis=1)

    def project(dz):
        s = ZS[dz]
        lhs = columns_of(dz)
        one = jnp.dot(lhs, q1[s].reshape(512, 256), preferred_element_type=F32)
        two = jnp.dot(lhs, q2[:, s].reshape(512, 256), preferred_element_type=F32)
        if dz == 0:
            acc1[...] = one
            acc2[...] = two
        else:
            acc1[...] += one
            acc2[...] += two

    def turned_pairs():
        table = cs[...]
        swapped = pltpu.roll(table, 64, 1)
        low = lax.broadcasted_iota(jnp.int32, (256, 128), 1) < 64
        return jnp.where(low, table, swapped), jnp.where(low, -swapped, table)

    def rope(e):
        cosine, sine = turned_pairs()
        return e * cosine + pltpu.roll(e, 64, 1) * sine

    def make_kv():
        raw = None
        for dz in DZ:
            term = jnp.dot(columns_of(dz), k2[:, ZS[dz]].reshape(512, 128), preferred_element_type=F32)
            raw = term if raw is None else raw + term
        acck[...] = raw
        raw = acck[...]
        kv[core, 384:640] = jnp.where(core == 0, rope(raw), raw).astype(BF16)

    def rope_queries():
        for h in range(4):
            e = acc1[:, 128 * h : 128 * h + 128] if h < 2 else acc2[:, 128 * (h - 2) : 128 * (h - 2) + 128]
            turned_e = rope(e).astype(BF16)
            for qb in (0, 1):
                qs[qb, h // 2, 128 * (h % 2) : 128 * (h % 2) + 128] = turned_e[128 * qb : 128 * qb + 128]

    def turn_values():
        eye = (
            lax.broadcasted_iota(jnp.int32, (128, 128), 0) == lax.broadcasted_iota(jnp.int32, (128, 128), 1)
        ).astype(F32).astype(BF16)
        vt[...] = lax.dot_general(eye, kv[1], (((1,), (1,)), ((), ())), preferred_element_type=F32).astype(BF16)

    def attend(qb, pair):
        keys = kv[0, 128 * qb : 128 * qb + 512]
        scores = lax.dot_general(keys, qs[qb, pair], (((1,), (1,)), ((), ())), preferred_element_type=F32)
        mask = bias[qb]
        scores = scores * (1.0 / math.sqrt(HD)) + jnp.concatenate([mask, mask], axis=1)
        expo = jnp.exp(scores - jnp.max(scores, axis=0, keepdims=True))
        denominator = jnp.sum(expo, axis=0, keepdims=True)
        summed = jnp.dot(vt[:, 128 * qb : 128 * qb + 512], expo.astype(BF16), preferred_element_type=F32)
        result = (summed / denominator).astype(BF16)
        for h in (0, 1):
            att[core, pair, qb, 128 * h : 128 * h + 128] = result[:, 128 * h : 128 * h + 128]

    def part_copy(dz, which, t, start):
        s = ZS[dz]
        zz = lax.rem(z + dz + 8, 8)
        goal = zz // 2
        here = (goal == x) & (core == t)
        sem = precv.at[core, x, lax.rem(zz, 2), which]
        land = rs.at[core, x, lax.rem(zz, 2), which]

        @pl.when(jnp.logical_not(here))
        def _():
            copy = remote(part.at[s, which, t], land, psend.at[s, which, t], sem, (chip * 2 + t, goal))
            copy.start() if start else copy.wait_send()

        if start:

            @pl.when(here)
            def _():
                pltpu.make_async_copy(part.at[s, which, t], land, sem).start()

    def out_project(dz, which):
        s = ZS[dz]
        dy = slice(2 * which, 2 * which + 2)
        weights = jnp.concatenate([att[:, :, 0].reshape(1024, 128), att[:, :, 1].reshape(1024, 128)], axis=1)
        total = jnp.dot(o1[s, dy].reshape(128, 384), weights[:384], preferred_element_type=F32)
        total += jnp.dot(o2[dy, s].reshape(128, 640), weights[384:], preferred_element_type=F32)
        total = total.astype(BF16)
        for t in (0, 1):
            part[s, which, t] = total[:, 128 * t : 128 * t + 128]
            part_copy(dz, which, t, True)

    def run(name):
        if name == "tables":
            tables()
        elif name == "place":
            place()
        elif name == "kv":
            make_kv()
        elif name == "rope":
            rope_queries()
        elif name == "vt":
            turn_values()
        elif name[0] == "A":
            attend(int(name[1]), int(name[2]))
        elif name[0] == "Q":
            project(int(name[1:]))
        else:
            dz, which = name[1:].split(",")
            out_project(int(dz), int(which))

    for _, _, kind, name in actions:
        if kind == "send":
            start_message(name)
        elif kind == "recv":
            finish_message(name)
        else:
            run(name)

    @pl.loop(1, 32)
    def _(by):
        row_copy(by).wait_send()

    kv_copy(0).wait_send()
    for m in messages:
        if m.name not in pseudo and m.name != "w3":
            copy_of(m).wait_send()
    for dz in DZ:
        for which in (0, 1):
            for t in (0, 1):
                part_copy(dz, which, t, False)
    for zz in (0, 1):
        sums = []
        for c in (0, 1):
            total = None
            for g in range(4):
                for which in (0, 1):
                    land = rs.at[c, g, zz, which]
                    remote(land, land, psend.at[0, 0, 0], precv.at[c, g, zz, which], across).wait_recv()
                term = rs[c, g, zz].reshape(256, 128).astype(F32)
                total = term if total is None else total + term
            sums.append(total)
        for dy in DY:
            s = YS[dy]
            block = jnp.concatenate([sums[0][64 * s : 64 * s + 64], sums[1][64 * s : 64 * s + 64]], axis=0)
            lane = pl.multiple_of((zz * 4 + lax.rem(y + dy + 4, 4)) * 128, 128)
            out[:, pl.ds(lane, 128)] = jnp.transpose(block).astype(BF16)


def per_device(tokens, context_row, lengths, qw, kw, vw, ow):
    nodes, actions, _ = plan()
    messages = [n for n in nodes if n.link != "core"]
    count = len(messages)
    dma = pltpu.SemaphoreType.DMA
    scratch = [
        pltpu.VMEM((4, 8, 128, 128), BF16),
        pltpu.VMEM((8, 4, 128, 256), BF16),
        pltpu.VMEM((4, 8, 128, 256), BF16),
        pltpu.VMEM((8, 4, 64, 384), BF16),
        pltpu.VMEM((4, 8, 64, 640), BF16),
        pltpu.VMEM((128, 1024), BF16),
        pltpu.VMEM((64, 128), jnp.int32),
        pltpu.VMEM((1, 64), jnp.int32),
        pltpu.VMEM((3072, 128), F32),
        pltpu.VMEM((32, 48, 128), BF16),
        pltpu.VMEM((32, 2, 48, 128), BF16),
        pltpu.VMEM((4, 2, 128, 1024), BF16),
        pltpu.VMEM((256, 128), F32),
        pltpu.VMEM((256, 256), F32),
        pltpu.VMEM((256, 256), F32),
        pltpu.VMEM((256, 128), F32),
        pltpu.VMEM((2, 512, 128), F32),
        pltpu.VMEM((2, 2, 256, 128), BF16),
        pltpu.VMEM((2, 640, 128), BF16),
        pltpu.VMEM((128, 640), BF16),
        pltpu.VMEM((2, 2, 2, 256, 128), BF16),
        pltpu.VMEM((8, 2, 2, 128, 128), BF16),
        pltpu.VMEM((2, 4, 2, 2, 128, 128), BF16),
        dma((9,)),
        dma((count,)),
        dma((count,)),
        dma((32,)),
        dma((32,)),
        dma((8, 2, 2)),
        dma((2, 4, 2, 2)),
    ]

    def body(*refs):
        kernel(messages, actions, *refs)

    return pl.pallas_call(
        body,
        out_shape=jax.ShapeDtypeStruct((128, 1024), BF16),
        in_specs=[pl.BlockSpec(memory_space=pltpu.HBM)] * 7,
        out_specs=pl.BlockSpec(memory_space=pltpu.VMEM),
        scratch_shapes=scratch,
        compiler_params=pltpu.CompilerParams(
            collective_id=0, has_side_effects=True, vmem_limit_bytes=63 * 2**20
        ),
    )(tokens, context_row.reshape(64, 128), lengths.reshape(1, 64), qw, kw, vw, ow.T)


def solution(mesh):
    return jax.shard_map(
        per_device,
        mesh=mesh,
        in_specs=(
            P("ctx", "head"),
            P(),
            P(),
            P("ctx", "head"),
            P("ctx", "head"),
            P("ctx", "head"),
            P("head", "ctx"),
        ),
        out_specs=P("ctx", "head"),
        check_vma=False,
    )
```

```python
import math

import jax
import jax.numpy as jnp
from jax import lax
from jax.experimental import pallas as pl
from jax.experimental.pallas import tpu as pltpu
from jax.sharding import PartitionSpec as P

MESH = pl.DeviceIdType.MESH
F32 = jnp.float32
BF16 = jnp.bfloat16
ROPE_BASE = 500000.0
HD = 128

DZ = (0, 1, -1, 2, -2, 3, -3, 4)
DY = (0, 1, -1, 2)
ZS = {d: i for i, d in enumerate(DZ)}
YS = {d: i for i, d in enumerate(DY)}
GROUPS = ((0, 1), (1, 3), (3, 5), (5, 7), (7, 8))
WIDE_GROUPS = ((0, 3), (3, 7), (7, 8))

LINK_RATE, LINK_LATENCY = 44, 3.2
PEER_RATE, PEER_LATENCY = 400.0, 1.0
AHEAD = 2.0
EXTRA = {"r": 6.0, "x": 1.0, "h": 1.0, "a": 0.5}


class Node:
    def __init__(self, name, link, deps, size, prio=(0,), src=None, dst=None):
        self.name, self.link, self.deps, self.size, self.prio = name, link, deps, size, prio
        self.src, self.dst = src, dst


def gather_messages(tag, rows, width1, width2, ready, rank, groups=GROUPS):
    out = []
    half = rows // 2
    size1 = rows * width1 * 2e-3
    size2 = rows * width2 * 2e-3
    full, top, bottom = (0, rows), (0, half), (half, half)

    def one(dz, dy, part):
        return (tag + "1", ZS[dz], YS[dy], part)

    def pair(dz, which):
        return (tag + "1", ZS[dz], (2 * which, 2), full)

    def two(dy, dz, part):
        return (tag + "2", YS[dy], ZS[dz], part)

    def group(dy, g):
        lo, hi = groups[g]
        return (tag + "2", YS[dy], (lo, hi - lo), full)

    def add(name, link, src, dst, deps, size, prio):
        out.append(Node(tag + name, link, [tag + d for d in deps] + ready, size, (rank,) + prio, src, dst))

    if width1:
        add("1y+1", "+y", one(0, 0, full), one(0, -1, full), [], size1, (0, 1))
        add("1y-1", "-y", one(0, 0, full), one(0, 1, full), [], size1, (0, 1))
        add("1y+2", "+y", one(0, -1, top), one(0, 2, top), ["1y+1"], size1 / 2, (0, 2))
        add("1y-2", "-y", one(0, 1, bottom), one(0, 2, bottom), ["1y-1"], size1 / 2, (0, 2))
    first = {0: ["1y-1"], 1: ["1y+1", "1y+2", "1y-2"]}
    for which in (0, 1) if width1 else ():
        for sign, link in ((1, "+z"), (-1, "-z")):
            mark = "+" if sign > 0 else "-"
            for step in (1, 2, 3, 4):
                if step == 4 and (sign > 0) != (which == 0):
                    continue
                deps = first[which] if step == 1 else [f"1z{which}{mark}{step - 1}"]
                far = 4 if step == 4 else -sign * step
                add(f"1z{which}{mark}{step}", link, pair(-sign * (step - 1), which), pair(far, which), deps,
                    2 * size1, (1, step))
    for sign, link in ((1, "+z"), (-1, "-z")):
        mark = "+" if sign > 0 else "-"
        for step in (1, 2, 3, 4):
            deps = [] if step == 1 else [f"2z{mark}{step - 1}"]
            part = full if step < 4 else (top if sign > 0 else bottom)
            far = 4 if step == 4 else -sign * step
            add(f"2z{mark}{step}", link, two(0, -sign * (step - 1), part), two(0, far, part), deps,
                size2 if step < 4 else size2 / 2, (0, step))
    for g, (lo, hi) in enumerate(groups):
        deps = []
        for dz in DZ[lo:hi]:
            deps += z_messages(dz)
        amount = size2 * (hi - lo)
        add(f"2y{g}+1", "+y", group(0, g), group(-1, g), deps, amount, (1, g))
        add(f"2y{g}-1", "-y", group(0, g), group(1, g), deps, amount, (1, g))
        if g % 2 == 0:
            add(f"2y{g}+2", "+y", group(-1, g), group(2, g), [f"2y{g}+1"], amount, (1, g))
        else:
            add(f"2y{g}-2", "-y", group(1, g), group(2, g), [f"2y{g}-1"], amount, (1, g))
    return out


def z_messages(dz):
    if dz == 0:
        return []
    return ["2z+4", "2z-4"] if dz == 4 else [f"2z{'+' if dz < 0 else '-'}{abs(dz)}"]


def needs(tag, dz, which, groups=GROUPS):
    g = [i for i, (lo, hi) in enumerate(groups) if lo <= ZS[dz] < hi][0]
    if which == 0:
        names = z_messages(dz) + [f"2y{g}-1"]
    else:
        names = [f"2y{g}+1", f"2y{g}+2" if g % 2 == 0 else f"2y{g}-2"]
    if tag != "k":
        if dz == 0:
            names += ["1y-1"] if which == 0 else ["1y+1", "1y+2", "1y-2"]
        elif dz == 4:
            names += ["1z0+4"] if which == 0 else ["1z1-4"]
        else:
            names += [f"1z{which}{'+' if dz < 0 else '-'}{abs(dz)}"]
    return [tag + n for n in names]


def all_nodes():
    x_all = ["x+a", "x+b", "x-a", "x-b", "xs+", "xs-", "xs2"]
    nodes = [
        Node("w1", "peer", [], 33),
        Node("w2", "peer", [], 33),
        Node("w3", "peer", [], 17),
        Node("r+z", "+z", [], 384, (-2,)),
        Node("r-z", "-z", [], 384, (-2,)),
        Node("r+y", "+y", [], 192, (-2,)),
        Node("r-y", "-y", [], 192, (-2,)),
        Node("rows", "peer", ["r+z", "r-z", "r+y", "r-y"], 384, (-1,)),
        Node("x+a", "+x", ["place"], 131, (0, 0)),
        Node("x+b", "+x", ["place"], 131, (0, 1)),
        Node("x-b", "-x", ["place"], 131, (0, 0)),
        Node("x-a", "-x", ["place"], 131, (0, 1)),
        Node("x+2", "+x", ["x+a"], 131, (0, 2)),
        Node("x-2", "-x", ["x-b"], 131, (0, 2)),
        Node("xs+", "peer", ["x+a", "x+b"], 262, (1,)),
        Node("xs-", "peer", ["x-a", "x-b"], 262, (1,)),
        Node("xs2", "peer", ["x+2", "x-2"], 262, (1,)),
        Node("h0", "peer", ["kv"], 65, (0,)),
        Node("h1", "+y", ["kv"], 85, (-1, 0)),
        Node("h2", "+y", ["kv"], 65, (-1, 1)),
        Node("h1s", "peer", ["h1"], 65, (0,)),
        Node("h2s", "peer", ["h2"], 33, (0,)),
    ]
    nodes += gather_messages("k", 128, 0, 128, ["w3"], 0, WIDE_GROUPS)
    nodes += gather_messages("q", 128, 256, 256, ["w1", "w2"], 1)
    nodes += gather_messages("o", 64, 384, 640, [], 2)

    def step(name, deps, span):
        nodes.append(Node(name, "core", deps, span, (len(nodes),)))

    step("tables", [], 1.5)
    step("place", ["rows"], 1.3)
    every = [n for dz in DZ for which in (0, 1) for n in needs("k", dz, which, WIDE_GROUPS)]
    step("kv", every + x_all + ["tables"], 1.0)
    for dz in DZ:
        step(f"Q{dz}", needs("q", dz, 0) + needs("q", dz, 1) + x_all, 0.45)
    step("rope", [f"Q{dz}" for dz in DZ] + ["tables"], 0.6)
    step("vt", ["h0", "h1", "h2", "h1s", "h2s"], 0.2)
    for qb in (0, 1):
        for pair in (0, 1):
            step(f"A{qb}{pair}", ["rope", "vt"], 0.8)
            nodes.append(Node(f"a{qb}{pair}", "peer", [f"A{qb}{pair}"], 65))
    for dz in DZ:
        for which in (0, 1):
            step(f"O{dz},{which}", needs("o", dz, which) + [f"a{qb}{pair}" for qb in (0, 1) for pair in (0, 1)], 0.3)
    return nodes


def plan():
    nodes = all_nodes()
    free, arrival, actions = {}, {}, []
    pending = list(nodes)
    while pending:
        best = None
        by_link = {}
        for m in pending:
            if all(d in arrival for d in m.deps):
                at = max([arrival[d] for d in m.deps], default=0.0)
                by_link.setdefault(m.link, []).append((at, m))
        for link, options in by_link.items():
            begin = max(free.get(link, 0.0), min(at for at, _ in options))
            at, m = min(((at, m) for at, m in options if at <= begin), key=lambda p: p[1].prio)
            if best is None or begin < best[0]:
                best = (begin, m, at)
        begin, m, at = best
        if m.link == "core":
            span, latency = m.size, 0.0
        elif m.link == "peer":
            span, latency = m.size / PEER_RATE, PEER_LATENCY
        else:
            span, latency = m.size / LINK_RATE, LINK_LATENCY
        latency += EXTRA.get(m.name[0], 0.0) if m.link != "core" and m.name != "rows" else 0.0
        free[m.link] = begin + span
        arrival[m.name] = begin + span + latency
        pending.remove(m)
        if m.link == "core":
            actions.append((begin, 2, "step", m.name))
        else:
            actions.append((max(at, begin - AHEAD), 1, "send", m.name))
            actions.append((arrival[m.name], 0, "recv", m.name))
    actions.sort(key=lambda a: a[:2])
    return nodes, actions, arrival


def kernel(messages, actions, tokens, table, lens, qw, kw, vw, ow, out,
           k2, q1, q2, o1, o2, tk, tb, ln, wide, rows_out, rows_in, xs, acck, acc1, acc2, cs, bias, qs, kv, vt, att, part, rs,
           lsem, send, recv, rsend, rrecv, psend, precv):
    ctx, x = lax.axis_index("ctx"), lax.axis_index("head")
    z, y, core = ctx // 8, (ctx // 2) % 4, ctx % 2
    chip = ctx // 2
    other = 1 - core
    buffers = {"k2": k2, "q1": q1, "q2": q2, "o1": o1, "o2": o2}
    number = {m.name: i for i, m in enumerate(messages)}

    def at(dz, dy, which, dx=0):
        return ((lax.rem(z + dz + 8, 8) * 4 + lax.rem(y + dy + 4, 4)) * 2 + which, lax.rem(x + dx + 4, 4))

    def chip_at(by, which):
        return (lax.rem(chip + by + 32, 32) * 2 + which, x)

    across = at(0, 0, other)
    mine = pl.ds(pl.multiple_of(core * 64, 64), 64)
    theirs = pl.ds(pl.multiple_of(other * 64, 64), 64)

    def columns(which, part):
        lo, n = ((0, 256), (256, 256))[part]
        return pl.ds(pl.multiple_of(which * 512 + lo, 128), n)

    def local(i, src, dst):
        return pltpu.make_async_copy(src, dst, lsem.at[i])

    own_kv = [local(7, kw, k2.at[0, 0, mine]), local(7, vw, k2.at[0, 0, mine])]
    early = [local(0, tokens, tk), local(1, table, tb), local(2, lens, ln)]
    late = [
        local(3, qw.at[:, columns(core, 0)], q1.at[0, 0, mine]),
        local(4, qw.at[:, columns(core, 1)], q2.at[0, 0, mine]),
        local(5, ow.at[:, pl.ds(0, 384)], o1.at[0, 0]),
        local(6, ow.at[:, pl.ds(384, 640)], o2.at[0, 0]),
    ]
    for copy in early + late:
        copy.start()
    for which in (0, 1):

        @pl.when(core == which)
        def _():
            own_kv[which].start()

    peers = [across] + [at(0, 0, which, dx) for dx in (1, 2, 3) for which in (0, 1)]
    peers += [chip_at(by, other) for by in (1, 2, -1, -2)]
    barrier = pltpu.get_barrier_semaphore()
    for peer in peers:
        pl.semaphore_signal(barrier, inc=1, device_id=peer, device_id_type=MESH)

    @pl.loop(1, 32)
    def _(by):
        pl.semaphore_signal(barrier, inc=1, device_id=chip_at(by, core), device_id_type=MESH)

    for copy in early:
        copy.wait()
    i0 = lax.broadcasted_iota(jnp.int32, (128, 128), 0)
    i1 = lax.broadcasted_iota(jnp.int32, (128, 128), 1)
    goal_row = jnp.broadcast_to((tb[pl.ds(ctx, 1), :] >> 7).astype(F32), (128, 128))
    goal_col = jnp.sum(jnp.where(i0 == i1, goal_row, 0.0), axis=1, keepdims=True)
    rank = jnp.sum(jnp.where((goal_col == goal_row) & (i0 < i1), 1.0, 0.0), axis=0, keepdims=True)
    slot = 3.0 * goal_row[:1] + rank
    pick = jnp.where(lax.broadcasted_iota(jnp.int32, (192, 128), 0).astype(F32) == slot, 1.0, 0.0).astype(BF16)
    picked = jnp.dot(pick, tk[...], preferred_element_type=F32)
    for j in range(8):
        wide[pl.ds(j, 192, stride=8), :] = picked[:, 128 * j : 128 * j + 128]
    rows_out[...] = wide[0:1536, :].astype(BF16).reshape(32, 48, 128)
    pl.semaphore_wait(barrier, len(peers) + 31)

    def row_copy(by, coming=False):
        goal, origin = lax.rem(chip + by, 32), lax.rem(chip + 32 - by, 32)
        src, dst = rows_out.at[goal], rows_in.at[chip, core]
        if coming:
            src = dst = rows_in.at[origin, core]
        return pltpu.make_async_remote_copy(
            src_ref=src, dst_ref=dst, send_sem=rsend.at[by], recv_sem=rrecv.at[by],
            device_id=chip_at(by, core), device_id_type=MESH,
        )

    @pl.loop(0, 31)
    def _(i):
        row_copy(1 + lax.rem(i + 15, 31)).start()

    keep = local(8, rows_out.at[chip], rows_in.at[chip, core])
    keep.start()
    for copy in late:
        copy.wait()
    own_kv[0].wait()

    x_low, x_high, x_far = lax.rem(x + 3, 4), lax.rem(x + 1, 4), lax.rem(x + 2, 4)
    top, bottom = pl.ds(0, 64), pl.ds(64, 64)
    far_keys, near_keys, own_keys, upper_keys = pl.ds(0, 128), pl.ds(128, 256), pl.ds(384, 256), pl.ds(512, 128)
    special = {
        "w1": (qw.at[:, columns(other, 0)], q1.at[0, 0, mine], q1.at[0, 0, theirs], across),
        "w2": (qw.at[:, columns(other, 1)], q2.at[0, 0, mine], q2.at[0, 0, theirs], across),
        "rows": (rows_in.at[:, core], rows_in.at[:, core], rows_in.at[:, other], across),
        "x+a": (xs.at[x, core, top], xs.at[x, core, top], xs.at[x_low, core, top], at(0, 0, core, 1)),
        "x+b": (xs.at[x, core, bottom], xs.at[x, core, bottom], xs.at[x_low, core, bottom], at(0, 0, core, 1)),
        "x-a": (xs.at[x, core, top], xs.at[x, core, top], xs.at[x_high, core, top], at(0, 0, core, -1)),
        "x-b": (xs.at[x, core, bottom], xs.at[x, core, bottom], xs.at[x_high, core, bottom], at(0, 0, core, -1)),
        "x+2": (xs.at[x_low, core, top], xs.at[x_low, core, top], xs.at[x_far, core, top], at(0, 0, core, 1)),
        "x-2": (xs.at[x_high, core, bottom], xs.at[x_high, core, bottom], xs.at[x_far, core, bottom],
                at(0, 0, core, -1)),
        "xs+": (xs.at[x_low, core], xs.at[x_low, core], xs.at[x_low, other], across),
        "xs-": (xs.at[x_high, core], xs.at[x_high, core], xs.at[x_high, other], across),
        "xs2": (xs.at[x_far, core], xs.at[x_far, core], xs.at[x_far, other], across),
        "h0": (kv.at[core, own_keys], kv.at[core, own_keys], kv.at[other, own_keys], across),
        "h1": (kv.at[core, own_keys], kv.at[core, near_keys], kv.at[core, near_keys], chip_at(1, core)),
        "h2": (kv.at[core, upper_keys], kv.at[core, far_keys], kv.at[core, far_keys], chip_at(2, core)),
        "h1s": (kv.at[core, near_keys], kv.at[core, near_keys], kv.at[other, near_keys], across),
        "h2s": (kv.at[core, far_keys], kv.at[core, far_keys], kv.at[other, far_keys], across),
    }
    for qb in (0, 1):
        for pair in (0, 1):
            special[f"a{qb}{pair}"] = (att.at[core, pair, qb], att.at[core, pair, qb], att.at[other, pair, qb], across)
    to = {"+z": at(1, 0, core), "-z": at(-1, 0, core), "+y": at(0, 1, core), "-y": at(0, -1, core)}

    def view(place):
        name, a, b, (lo, n) = place
        b = pl.ds(*b) if isinstance(b, tuple) else b
        return buffers[name].at[a, b, pl.ds(lo, n)]

    def remote(src, dst, ssem, rsem, device):
        return pltpu.make_async_remote_copy(
            src_ref=src, dst_ref=dst, send_sem=ssem, recv_sem=rsem, device_id=device, device_id_type=MESH
        )

    def copy_of(m, coming=False):
        i = number[m.name]
        if m.name in special:
            src, dst, land, device = special[m.name]
        else:
            src, dst, land, device = view(m.src), view(m.dst), view(m.dst), to[m.link]
        if coming:
            src = dst = land
        return remote(src, dst, send.at[i], recv.at[i], device)

    by_name = {m.name: m for m in messages}

    def kv_copy(which):
        i = number["w3"]
        src = (vw, kw)[which]
        return remote(src, k2.at[0, 0, mine], send.at[i], recv.at[i], across)

    def place():
        t = tb[...]
        upper = jnp.where(i0 < i1, 1.0, 0.0).astype(BF16)
        landing = []
        for half in (0, 1):
            here = (t >> 7) == 2 * chip + half
            nth = jnp.dot(jnp.where(here, 1.0, 0.0).astype(BF16), upper, preferred_element_type=F32)
            row = ((t & 255) + 1).astype(F32)
            for k in range(3):
                landing.append(jnp.sum(jnp.where(here & (nth == float(k)), row, 0.0), axis=1, keepdims=True))
        goal = jnp.concatenate(landing, axis=0)
        lane = lax.broadcasted_iota(jnp.int32, (384, 256), 1).astype(F32) + 1.0
        spot = jnp.transpose(jnp.where(goal == lane, 1.0, 0.0)).astype(BF16)
        wide[...] = rows_in[...].astype(F32).reshape(3072, 128)
        for j in range(8):
            rows = [wide[pl.ds(8 * n + j, 64, stride=48), :] for n in range(6)]
            rows = jnp.concatenate(rows, axis=0).astype(BF16)
            found = jnp.dot(spot, rows, preferred_element_type=F32).astype(BF16)
            xs[x, :, :, 128 * j : 128 * j + 128] = found.reshape(2, 128, 128)

    pseudo = ("r+z", "r-z", "r+y", "r-y")

    def start_message(name):
        if name == "rows":
            keep.wait()

            @pl.loop(1, 32)
            def _(by):
                row_copy(by, True).wait_recv()

        if name == "w3":
            for which in (0, 1):

                @pl.when(core == which)
                def _():
                    kv_copy(which).start()

        elif name not in pseudo:
            copy_of(by_name[name]).start()

    def finish_message(name):
        if name == "w3":
            i = number["w3"]
            land = k2.at[0, 0, theirs]
            remote(land, land, send.at[i], recv.at[i], across).wait_recv()
        elif name not in pseudo:
            copy_of(by_name[name], True).wait_recv()

    def tables():
        base = chip * 256
        d0 = lax.broadcasted_iota(jnp.int32, (64, 64), 0)
        d1 = lax.broadcasted_iota(jnp.int32, (64, 64), 1)
        spread = jnp.broadcast_to(ln[...].astype(F32), (64, 64))
        end_col = jnp.sum(jnp.where(d1 <= d0, spread, 0.0), axis=1, keepdims=True)
        len_col = jnp.sum(jnp.where(d1 == d0, spread, 0.0), axis=1, keepdims=True)
        end_row = jnp.sum(jnp.where(d0 <= d1, jnp.broadcast_to(len_col, (64, 64)), 0.0), axis=0, keepdims=True)
        row_id = (base + lax.broadcasted_iota(jnp.int32, (64, 256), 1)).astype(F32)
        before = row_id >= end_col
        q_doc = jnp.sum(jnp.where(before, 1.0, 0.0), axis=0, keepdims=True)
        position = row_id - jnp.sum(jnp.where(before, len_col, 0.0), axis=0, keepdims=True)
        turn = lax.broadcasted_iota(jnp.int32, (64, 256), 0).astype(F32)
        angle = position * jnp.exp(turn * (-2.0 / HD * math.log(ROPE_BASE)))
        cs[...] = jnp.transpose(jnp.concatenate([jnp.cos(angle), jnp.sin(angle)], axis=0))
        key_id = base - 384 + lax.broadcasted_iota(jnp.int32, (640, 64), 0)
        k_doc = jnp.sum(jnp.where(key_id.astype(F32) >= end_row, 1.0, 0.0), axis=1, keepdims=True)
        for qb in (0, 1):
            lo = 128 * qb
            kid = base - 384 + lo + lax.broadcasted_iota(jnp.int32, (512, 128), 0)
            qid = base + lo + lax.broadcasted_iota(jnp.int32, (512, 128), 1)
            allowed = (k_doc[lo : lo + 512] == q_doc[:, lo : lo + 128]) & (kid <= qid) & (kid >= 0)
            bias[qb] = jnp.where(allowed, 0.0, -jnp.inf)

    def columns_of(dz):
        zz = lax.rem(z + dz + 8, 8)
        parts = []
        for dy in DY:
            lane = pl.multiple_of((lax.rem(zz, 2) * 4 + lax.rem(y + dy + 4, 4)) * 128, 128)
            parts.append(xs[zz // 2, :, :, pl.ds(lane, 128)].reshape(256, 128))
        return jnp.concatenate(parts, axis=1)

    def project(dz):
        s = ZS[dz]
        lhs = columns_of(dz)
        one = jnp.dot(lhs, q1[s].reshape(512, 256), preferred_element_type=F32)
        two = jnp.dot(lhs, q2[:, s].reshape(512, 256), preferred_element_type=F32)
        if dz == 0:
            acc1[...] = one
            acc2[...] = two
        else:
            acc1[...] += one
            acc2[...] += two

    def turned_pairs():
        table = cs[...]
        swapped = pltpu.roll(table, 64, 1)
        low = lax.broadcasted_iota(jnp.int32, (256, 128), 1) < 64
        return jnp.where(low, table, swapped), jnp.where(low, -swapped, table)

    def rope(e):
        cosine, sine = turned_pairs()
        return e * cosine + pltpu.roll(e, 64, 1) * sine

    def make_kv():
        raw = None
        for dz in DZ:
            term = jnp.dot(columns_of(dz), k2[:, ZS[dz]].reshape(512, 128), preferred_element_type=F32)
            raw = term if raw is None else raw + term
        acck[...] = raw
        raw = acck[...]
        kv[core, 384:640] = jnp.where(core == 0, rope(raw), raw).astype(BF16)

    def rope_queries():
        for h in range(4):
            e = acc1[:, 128 * h : 128 * h + 128] if h < 2 else acc2[:, 128 * (h - 2) : 128 * (h - 2) + 128]
            turned_e = rope(e).astype(BF16)
            for qb in (0, 1):
                qs[qb, h // 2, 128 * (h % 2) : 128 * (h % 2) + 128] = turned_e[128 * qb : 128 * qb + 128]

    def turn_values():
        eye = (
            lax.broadcasted_iota(jnp.int32, (128, 128), 0) == lax.broadcasted_iota(jnp.int32, (128, 128), 1)
        ).astype(F32).astype(BF16)
        vt[...] = lax.dot_general(eye, kv[1], (((1,), (1,)), ((), ())), preferred_element_type=F32).astype(BF16)

    def attend(qb, pair):
        keys = kv[0, 128 * qb : 128 * qb + 512]
        scores = lax.dot_general(keys, qs[qb, pair], (((1,), (1,)), ((), ())), preferred_element_type=F32)
        mask = bias[qb]
        scores = scores * (1.0 / math.sqrt(HD)) + jnp.concatenate([mask, mask], axis=1)
        expo = jnp.exp(scores - jnp.max(scores, axis=0, keepdims=True))
        denominator = jnp.sum(expo, axis=0, keepdims=True)
        summed = jnp.dot(vt[:, 128 * qb : 128 * qb + 512], expo.astype(BF16), preferred_element_type=F32)
        result = (summed / denominator).astype(BF16)
        for h in (0, 1):
            att[core, pair, qb, 128 * h : 128 * h + 128] = result[:, 128 * h : 128 * h + 128]

    def part_copy(dz, which, t, start):
        s = ZS[dz]
        zz = lax.rem(z + dz + 8, 8)
        goal = zz // 2
        here = (goal == x) & (core == t)
        sem = precv.at[core, x, lax.rem(zz, 2), which]
        land = rs.at[core, x, lax.rem(zz, 2), which]

        @pl.when(jnp.logical_not(here))
        def _():
            copy = remote(part.at[s, which, t], land, psend.at[s, which, t], sem, (chip * 2 + t, goal))
            copy.start() if start else copy.wait_send()

        if start:

            @pl.when(here)
            def _():
                pltpu.make_async_copy(part.at[s, which, t], land, sem).start()

    def out_project(dz, which):
        s = ZS[dz]
        dy = slice(2 * which, 2 * which + 2)
        weights = jnp.concatenate([att[:, :, 0].reshape(1024, 128), att[:, :, 1].reshape(1024, 128)], axis=1)
        total = jnp.dot(o1[s, dy].reshape(128, 384), weights[:384], preferred_element_type=F32)
        total += jnp.dot(o2[dy, s].reshape(128, 640), weights[384:], preferred_element_type=F32)
        total = total.astype(BF16)
        for t in (0, 1):
            part[s, which, t] = total[:, 128 * t : 128 * t + 128]
            part_copy(dz, which, t, True)

    def run(name):
        if name == "tables":
            tables()
        elif name == "place":
            place()
        elif name == "kv":
            make_kv()
        elif name == "rope":
            rope_queries()
        elif name == "vt":
            turn_values()
        elif name[0] == "A":
            attend(int(name[1]), int(name[2]))
        elif name[0] == "Q":
            project(int(name[1:]))
        else:
            dz, which = name[1:].split(",")
            out_project(int(dz), int(which))

    for _, _, kind, name in actions:
        if kind == "send":
            start_message(name)
        elif kind == "recv":
            finish_message(name)
        else:
            run(name)

    @pl.loop(1, 32)
    def _(by):
        row_copy(by).wait_send()

    kv_copy(0).wait_send()
    for m in messages:
        if m.name not in pseudo and m.name != "w3":
            copy_of(m).wait_send()
    for dz in DZ:
        for which in (0, 1):
            for t in (0, 1):
                part_copy(dz, which, t, False)
    for zz in (0, 1):
        sums = []
        for c in (0, 1):
            total = None
            for g in range(4):
                for which in (0, 1):
                    land = rs.at[c, g, zz, which]
                    remote(land, land, psend.at[0, 0, 0], precv.at[c, g, zz, which], across).wait_recv()
                term = rs[c, g, zz].reshape(256, 128).astype(F32)
                total = term if total is None else total + term
            sums.append(total)
        for dy in DY:
            s = YS[dy]
            block = jnp.concatenate([sums[0][64 * s : 64 * s + 64], sums[1][64 * s : 64 * s + 64]], axis=0)
            lane = pl.multiple_of((zz * 4 + lax.rem(y + dy + 4, 4)) * 128, 128)
            out[:, pl.ds(lane, 128)] = jnp.transpose(block).astype(BF16)


def per_device(tokens, context_row, lengths, qw, kw, vw, ow):
    nodes, actions, _ = plan()
    messages = [n for n in nodes if n.link != "core"]
    count = len(messages)
    dma = pltpu.SemaphoreType.DMA
    scratch = [
        pltpu.VMEM((4, 8, 128, 128), BF16),
        pltpu.VMEM((8, 4, 128, 256), BF16),
        pltpu.VMEM((4, 8, 128, 256), BF16),
        pltpu.VMEM((8, 4, 64, 384), BF16),
        pltpu.VMEM((4, 8, 64, 640), BF16),
        pltpu.VMEM((128, 1024), BF16),
        pltpu.VMEM((64, 128), jnp.int32),
        pltpu.VMEM((1, 64), jnp.int32),
        pltpu.VMEM((3072, 128), F32),
        pltpu.VMEM((32, 48, 128), BF16),
        pltpu.VMEM((32, 2, 48, 128), BF16),
        pltpu.VMEM((4, 2, 128, 1024), BF16),
        pltpu.VMEM((256, 128), F32),
        pltpu.VMEM((256, 256), F32),
        pltpu.VMEM((256, 256), F32),
        pltpu.VMEM((256, 128), F32),
        pltpu.VMEM((2, 512, 128), F32),
        pltpu.VMEM((2, 2, 256, 128), BF16),
        pltpu.VMEM((2, 640, 128), BF16),
        pltpu.VMEM((128, 640), BF16),
        pltpu.VMEM((2, 2, 2, 256, 128), BF16),
        pltpu.VMEM((8, 2, 2, 128, 128), BF16),
        pltpu.VMEM((2, 4, 2, 2, 128, 128), BF16),
        dma((9,)),
        dma((count,)),
        dma((count,)),
        dma((32,)),
        dma((32,)),
        dma((8, 2, 2)),
        dma((2, 4, 2, 2)),
    ]

    def body(*refs):
        kernel(messages, actions, *refs)

    return pl.pallas_call(
        body,
        out_shape=pltpu.VMEM((128, 1024), BF16),
        in_specs=[pl.BlockSpec(memory_space=pltpu.HBM)] * 7,
        out_specs=pl.BlockSpec(memory_space=pltpu.VMEM),
        scratch_shapes=scratch,
        compiler_params=pltpu.CompilerParams(
            collective_id=0, has_side_effects=True, vmem_limit_bytes=63 * 2**20
        ),
    )(tokens, context_row.reshape(64, 128), lengths.reshape(1, 64), qw, kw, vw, ow.T)


def solution(mesh):
    return jax.shard_map(
        per_device,
        mesh=mesh,
        in_specs=(
            P("ctx", "head"),
            P(),
            P(),
            P("ctx", "head"),
            P("ctx", "head"),
            P("ctx", "head"),
            P("head", "ctx"),
        ),
        out_specs=P("ctx", "head"),
        check_vma=False,
    )
```

```python
import math

import jax
import jax.numpy as jnp
from jax import lax
from jax.experimental import pallas as pl
from jax.experimental.pallas import tpu as pltpu
from jax.sharding import PartitionSpec as P

MESH = pl.DeviceIdType.MESH
F32 = jnp.float32
BF16 = jnp.bfloat16
ROPE_BASE = 500000.0
HD = 128

DZ = (0, 1, -1, 2, -2, 3, -3, 4)
DY = (0, 1, -1, 2)
ZS = {d: i for i, d in enumerate(DZ)}
YS = {d: i for i, d in enumerate(DY)}
GROUPS = ((0, 1), (1, 3), (3, 5), (5, 7), (7, 8))
WIDE_GROUPS = ((0, 3), (3, 7), (7, 8))

LINK_RATE, LINK_LATENCY = 44, 3.2
PEER_RATE, PEER_LATENCY = 400.0, 1.0
AHEAD = 2.0
EXTRA = {"r": 6.0, "x": 1.0, "h": 1.0, "a": 0.5}


class Node:
    def __init__(self, name, link, deps, size, prio=(0,), src=None, dst=None):
        self.name, self.link, self.deps, self.size, self.prio = name, link, deps, size, prio
        self.src, self.dst = src, dst


def gather_messages(tag, rows, width1, width2, ready, rank, groups=GROUPS):
    out = []
    half = rows // 2
    size1 = rows * width1 * 2e-3
    size2 = rows * width2 * 2e-3
    full, top, bottom = (0, rows), (0, half), (half, half)

    def one(dz, dy, part):
        return (tag + "1", ZS[dz], YS[dy], part)

    def pair(dz, which):
        return (tag + "1", ZS[dz], (2 * which, 2), full)

    def two(dy, dz, part):
        return (tag + "2", YS[dy], ZS[dz], part)

    def group(dy, g):
        lo, hi = groups[g]
        return (tag + "2", YS[dy], (lo, hi - lo), full)

    def add(name, link, src, dst, deps, size, prio):
        out.append(Node(tag + name, link, [tag + d for d in deps] + ready, size, (rank,) + prio, src, dst))

    if width1:
        add("1y+1", "+y", one(0, 0, full), one(0, -1, full), [], size1, (0, 1))
        add("1y-1", "-y", one(0, 0, full), one(0, 1, full), [], size1, (0, 1))
        add("1y+2", "+y", one(0, -1, top), one(0, 2, top), ["1y+1"], size1 / 2, (0, 2))
        add("1y-2", "-y", one(0, 1, bottom), one(0, 2, bottom), ["1y-1"], size1 / 2, (0, 2))
    first = {0: ["1y-1"], 1: ["1y+1", "1y+2", "1y-2"]}
    for which in (0, 1) if width1 else ():
        for sign, link in ((1, "+z"), (-1, "-z")):
            mark = "+" if sign > 0 else "-"
            for step in (1, 2, 3, 4):
                if step == 4 and (sign > 0) != (which == 0):
                    continue
                deps = first[which] if step == 1 else [f"1z{which}{mark}{step - 1}"]
                far = 4 if step == 4 else -sign * step
                add(f"1z{which}{mark}{step}", link, pair(-sign * (step - 1), which), pair(far, which), deps,
                    2 * size1, (1, step))
    for sign, link in ((1, "+z"), (-1, "-z")):
        mark = "+" if sign > 0 else "-"
        for step in (1, 2, 3, 4):
            deps = [] if step == 1 else [f"2z{mark}{step - 1}"]
            part = full if step < 4 else (top if sign > 0 else bottom)
            far = 4 if step == 4 else -sign * step
            add(f"2z{mark}{step}", link, two(0, -sign * (step - 1), part), two(0, far, part), deps,
                size2 if step < 4 else size2 / 2, (0, step))
    for g, (lo, hi) in enumerate(groups):
        deps = []
        for dz in DZ[lo:hi]:
            deps += z_messages(dz)
        amount = size2 * (hi - lo)
        add(f"2y{g}+1", "+y", group(0, g), group(-1, g), deps, amount, (1, g))
        add(f"2y{g}-1", "-y", group(0, g), group(1, g), deps, amount, (1, g))
        if g % 2 == 0:
            add(f"2y{g}+2", "+y", group(-1, g), group(2, g), [f"2y{g}+1"], amount, (1, g))
        else:
            add(f"2y{g}-2", "-y", group(1, g), group(2, g), [f"2y{g}-1"], amount, (1, g))
    return out


def z_messages(dz):
    if dz == 0:
        return []
    return ["2z+4", "2z-4"] if dz == 4 else [f"2z{'+' if dz < 0 else '-'}{abs(dz)}"]


def needs(tag, dz, which, groups=GROUPS):
    g = [i for i, (lo, hi) in enumerate(groups) if lo <= ZS[dz] < hi][0]
    if which == 0:
        names = z_messages(dz) + [f"2y{g}-1"]
    else:
        names = [f"2y{g}+1", f"2y{g}+2" if g % 2 == 0 else f"2y{g}-2"]
    if tag != "k":
        if dz == 0:
            names += ["1y-1"] if which == 0 else ["1y+1", "1y+2", "1y-2"]
        elif dz == 4:
            names += ["1z0+4"] if which == 0 else ["1z1-4"]
        else:
            names += [f"1z{which}{'+' if dz < 0 else '-'}{abs(dz)}"]
    return [tag + n for n in names]


def all_nodes():
    x_all = ["x+a", "x+b", "x-a", "x-b", "xs+", "xs-", "xs2"]
    nodes = [
        Node("w1", "peer", [], 33),
        Node("w2", "peer", [], 33),
        Node("w3", "peer", [], 17),
        Node("r+z", "+z", [], 384, (-2,)),
        Node("r-z", "-z", [], 384, (-2,)),
        Node("r+y", "+y", [], 192, (-2,)),
        Node("r-y", "-y", [], 192, (-2,)),
        Node("rows", "peer", ["r+z", "r-z", "r+y", "r-y"], 384, (-1,)),
        Node("x+a", "+x", ["place"], 131, (0, 0)),
        Node("x+b", "+x", ["place"], 131, (0, 1)),
        Node("x-b", "-x", ["place"], 131, (0, 0)),
        Node("x-a", "-x", ["place"], 131, (0, 1)),
        Node("x+2", "+x", ["x+a"], 131, (0, 2)),
        Node("x-2", "-x", ["x-b"], 131, (0, 2)),
        Node("xs+", "peer", ["x+a", "x+b"], 262, (1,)),
        Node("xs-", "peer", ["x-a", "x-b"], 262, (1,)),
        Node("xs2", "peer", ["x+2", "x-2"], 262, (1,)),
        Node("h0", "peer", ["kv"], 65, (0,)),
        Node("h1", "+y", ["kv"], 85, (-1, 0)),
        Node("h2", "+y", ["kv"], 65, (-1, 1)),
        Node("h1s", "peer", ["h1"], 65, (0,)),
        Node("h2s", "peer", ["h2"], 33, (0,)),
    ]
    nodes += gather_messages("k", 128, 0, 128, ["w3"], 0, WIDE_GROUPS)
    nodes += gather_messages("q", 128, 256, 256, ["w1", "w2"], 1)
    nodes += gather_messages("o", 64, 384, 640, [], 2)

    def step(name, deps, span):
        nodes.append(Node(name, "core", deps, span, (len(nodes),)))

    step("tables", [], 1.5)
    step("place", ["rows"], 1.3)
    every = [n for dz in DZ for which in (0, 1) for n in needs("k", dz, which, WIDE_GROUPS)]
    step("kv", every + x_all + ["tables"], 1.0)
    for dz in DZ:
        step(f"Q{dz}", needs("q", dz, 0) + needs("q", dz, 1) + x_all, 0.45)
    step("rope", [f"Q{dz}" for dz in DZ] + ["tables"], 0.6)
    step("vt", ["h0", "h1", "h2", "h1s", "h2s"], 0.2)
    for qb in (0, 1):
        for pair in (0, 1):
            step(f"A{qb}{pair}", ["rope", "vt"], 0.8)
            nodes.append(Node(f"a{qb}{pair}", "peer", [f"A{qb}{pair}"], 65))
    for dz in DZ:
        for which in (0, 1):
            step(f"O{dz},{which}", needs("o", dz, which) + [f"a{qb}{pair}" for qb in (0, 1) for pair in (0, 1)], 0.3)
    return nodes


def plan():
    nodes = all_nodes()
    free, arrival, actions = {}, {}, []
    pending = list(nodes)
    while pending:
        best = None
        by_link = {}
        for m in pending:
            if all(d in arrival for d in m.deps):
                at = max([arrival[d] for d in m.deps], default=0.0)
                by_link.setdefault(m.link, []).append((at, m))
        for link, options in by_link.items():
            begin = max(free.get(link, 0.0), min(at for at, _ in options))
            at, m = min(((at, m) for at, m in options if at <= begin), key=lambda p: p[1].prio)
            if best is None or begin < best[0]:
                best = (begin, m, at)
        begin, m, at = best
        if m.link == "core":
            span, latency = m.size, 0.0
        elif m.link == "peer":
            span, latency = m.size / PEER_RATE, PEER_LATENCY
        else:
            span, latency = m.size / LINK_RATE, LINK_LATENCY
        latency += EXTRA.get(m.name[0], 0.0) if m.link != "core" and m.name != "rows" else 0.0
        free[m.link] = begin + span
        arrival[m.name] = begin + span + latency
        pending.remove(m)
        if m.link == "core":
            actions.append((begin, 2, "step", m.name))
        else:
            actions.append((max(at, begin - AHEAD), 1, "send", m.name))
            actions.append((arrival[m.name], 0, "recv", m.name))
    actions.sort(key=lambda a: a[:2])
    return nodes, actions, arrival


def kernel(messages, actions, tokens, table, lens, qw, kw, vw, ow, out,
           k2, q1, q2, o1, o2, tk, tb, ln, wide, rows_out, rows_in, xs, acck, acc1, acc2, cs, bias, qs, kv, vt, att, part, rs,
           lsem, send, recv, rsend, rrecv, psend, precv):
    ctx, x = lax.axis_index("ctx"), lax.axis_index("head")
    z, y, core = ctx // 8, (ctx // 2) % 4, ctx % 2
    chip = ctx // 2
    other = 1 - core
    buffers = {"k2": k2, "q1": q1, "q2": q2, "o1": o1, "o2": o2}
    number = {m.name: i for i, m in enumerate(messages)}

    def at(dz, dy, which, dx=0):
        return ((lax.rem(z + dz + 8, 8) * 4 + lax.rem(y + dy + 4, 4)) * 2 + which, lax.rem(x + dx + 4, 4))

    def chip_at(by, which):
        return (lax.rem(chip + by + 32, 32) * 2 + which, x)

    across = at(0, 0, other)
    mine = pl.ds(pl.multiple_of(core * 64, 64), 64)
    theirs = pl.ds(pl.multiple_of(other * 64, 64), 64)

    def columns(which, part):
        lo, n = ((0, 256), (256, 256))[part]
        return pl.ds(pl.multiple_of(which * 512 + lo, 128), n)

    def local(i, src, dst):
        return pltpu.make_async_copy(src, dst, lsem.at[i])

    own_kv = [local(7, kw, k2.at[0, 0, mine]), local(7, vw, k2.at[0, 0, mine])]
    early = [local(0, tokens, tk), local(1, table, tb), local(2, lens, ln)]
    late = [
        local(3, qw.at[:, columns(core, 0)], q1.at[0, 0, mine]),
        local(4, qw.at[:, columns(core, 1)], q2.at[0, 0, mine]),
        local(5, ow.at[:, pl.ds(0, 384)], o1.at[0, 0]),
        local(6, ow.at[:, pl.ds(384, 640)], o2.at[0, 0]),
    ]
    for copy in early + late:
        copy.start()
    for which in (0, 1):

        @pl.when(core == which)
        def _():
            own_kv[which].start()

    peers = [across] + [at(0, 0, which, dx) for dx in (1, 2, 3) for which in (0, 1)]
    peers += [chip_at(by, other) for by in (1, 2, -1, -2)]
    barrier = pltpu.get_barrier_semaphore()
    for peer in peers:
        pl.semaphore_signal(barrier, inc=1, device_id=peer, device_id_type=MESH)

    @pl.loop(1, 32)
    def _(by):
        pl.semaphore_signal(barrier, inc=1, device_id=chip_at(by, core), device_id_type=MESH)

    for copy in early:
        copy.wait()
    i0 = lax.broadcasted_iota(jnp.int32, (128, 128), 0)
    i1 = lax.broadcasted_iota(jnp.int32, (128, 128), 1)
    goal_row = jnp.broadcast_to((tb[pl.ds(ctx, 1), :] >> 7).astype(F32), (128, 128))
    goal_col = jnp.sum(jnp.where(i0 == i1, goal_row, 0.0), axis=1, keepdims=True)
    rank = jnp.sum(jnp.where((goal_col == goal_row) & (i0 < i1), 1.0, 0.0), axis=0, keepdims=True)
    slot = 3.0 * goal_row[:1] + rank
    pick = jnp.where(lax.broadcasted_iota(jnp.int32, (192, 128), 0).astype(F32) == slot, 1.0, 0.0).astype(BF16)
    picked = jnp.dot(pick, tk[...], preferred_element_type=F32)
    for j in range(8):
        wide[pl.ds(j, 192, stride=8), :] = picked[:, 128 * j : 128 * j + 128]
    rows_out[...] = wide[0:1536, :].astype(BF16).reshape(32, 48, 128)
    pl.semaphore_wait(barrier, len(peers) + 31)

    def row_copy(by, coming=False):
        goal, origin = lax.rem(chip + by, 32), lax.rem(chip + 32 - by, 32)
        src, dst = rows_out.at[goal], rows_in.at[chip, core]
        if coming:
            src = dst = rows_in.at[origin, core]
        return pltpu.make_async_remote_copy(
            src_ref=src, dst_ref=dst, send_sem=rsend.at[by], recv_sem=rrecv.at[by],
            device_id=chip_at(by, core), device_id_type=MESH,
        )

    @pl.loop(0, 31)
    def _(i):
        row_copy(1 + lax.rem(i + 15, 31)).start()

    keep = local(8, rows_out.at[chip], rows_in.at[chip, core])
    keep.start()
    for copy in late:
        copy.wait()
    own_kv[0].wait()

    x_low, x_high, x_far = lax.rem(x + 3, 4), lax.rem(x + 1, 4), lax.rem(x + 2, 4)
    top, bottom = pl.ds(0, 64), pl.ds(64, 64)
    far_keys, near_keys, own_keys, upper_keys = pl.ds(0, 128), pl.ds(128, 256), pl.ds(384, 256), pl.ds(512, 128)
    special = {
        "w1": (qw.at[:, columns(other, 0)], q1.at[0, 0, mine], q1.at[0, 0, theirs], across),
        "w2": (qw.at[:, columns(other, 1)], q2.at[0, 0, mine], q2.at[0, 0, theirs], across),
        "rows": (rows_in.at[:, core], rows_in.at[:, core], rows_in.at[:, other], across),
        "x+a": (xs.at[x, core, top], xs.at[x, core, top], xs.at[x_low, core, top], at(0, 0, core, 1)),
        "x+b": (xs.at[x, core, bottom], xs.at[x, core, bottom], xs.at[x_low, core, bottom], at(0, 0, core, 1)),
        "x-a": (xs.at[x, core, top], xs.at[x, core, top], xs.at[x_high, core, top], at(0, 0, core, -1)),
        "x-b": (xs.at[x, core, bottom], xs.at[x, core, bottom], xs.at[x_high, core, bottom], at(0, 0, core, -1)),
        "x+2": (xs.at[x_low, core, top], xs.at[x_low, core, top], xs.at[x_far, core, top], at(0, 0, core, 1)),
        "x-2": (xs.at[x_high, core, bottom], xs.at[x_high, core, bottom], xs.at[x_far, core, bottom],
                at(0, 0, core, -1)),
        "xs+": (xs.at[x_low, core], xs.at[x_low, core], xs.at[x_low, other], across),
        "xs-": (xs.at[x_high, core], xs.at[x_high, core], xs.at[x_high, other], across),
        "xs2": (xs.at[x_far, core], xs.at[x_far, core], xs.at[x_far, other], across),
        "h0": (kv.at[core, own_keys], kv.at[core, own_keys], kv.at[other, own_keys], across),
        "h1": (kv.at[core, own_keys], kv.at[core, near_keys], kv.at[core, near_keys], chip_at(1, core)),
        "h2": (kv.at[core, upper_keys], kv.at[core, far_keys], kv.at[core, far_keys], chip_at(2, core)),
        "h1s": (kv.at[core, near_keys], kv.at[core, near_keys], kv.at[other, near_keys], across),
        "h2s": (kv.at[core, far_keys], kv.at[core, far_keys], kv.at[other, far_keys], across),
    }
    for qb in (0, 1):
        for pair in (0, 1):
            special[f"a{qb}{pair}"] = (att.at[core, pair, qb], att.at[core, pair, qb], att.at[other, pair, qb], across)
    to = {"+z": at(1, 0, core), "-z": at(-1, 0, core), "+y": at(0, 1, core), "-y": at(0, -1, core)}

    def view(place):
        name, a, b, (lo, n) = place
        b = pl.ds(*b) if isinstance(b, tuple) else b
        return buffers[name].at[a, b, pl.ds(lo, n)]

    def remote(src, dst, ssem, rsem, device):
        return pltpu.make_async_remote_copy(
            src_ref=src, dst_ref=dst, send_sem=ssem, recv_sem=rsem, device_id=device, device_id_type=MESH
        )

    def copy_of(m, coming=False):
        i = number[m.name]
        if m.name in special:
            src, dst, land, device = special[m.name]
        else:
            src, dst, land, device = view(m.src), view(m.dst), view(m.dst), to[m.link]
        if coming:
            src = dst = land
        return remote(src, dst, send.at[i], recv.at[i], device)

    by_name = {m.name: m for m in messages}

    def kv_copy(which):
        i = number["w3"]
        src = (vw, kw)[which]
        return remote(src, k2.at[0, 0, mine], send.at[i], recv.at[i], across)

    def place():
        t = tb[...]
        upper = jnp.where(i0 < i1, 1.0, 0.0).astype(BF16)
        landing = []
        for half in (0, 1):
            here = (t >> 7) == 2 * chip + half
            nth = jnp.dot(jnp.where(here, 1.0, 0.0).astype(BF16), upper, preferred_element_type=F32)
            row = ((t & 255) + 1).astype(F32)
            for k in range(3):
                landing.append(jnp.sum(jnp.where(here & (nth == float(k)), row, 0.0), axis=1, keepdims=True))
        goal = jnp.concatenate(landing, axis=0)
        lane = lax.broadcasted_iota(jnp.int32, (384, 256), 1).astype(F32) + 1.0
        spot = jnp.transpose(jnp.where(goal == lane, 1.0, 0.0)).astype(BF16)
        wide[...] = rows_in[...].astype(F32).reshape(3072, 128)
        for j in range(8):
            rows = [wide[pl.ds(8 * n + j, 64, stride=48), :] for n in range(6)]
            rows = jnp.concatenate(rows, axis=0).astype(BF16)
            found = jnp.dot(spot, rows, preferred_element_type=F32).astype(BF16)
            xs[x, :, :, 128 * j : 128 * j + 128] = found.reshape(2, 128, 128)

    pseudo = ("r+z", "r-z", "r+y", "r-y")

    def start_message(name):
        if name == "rows":
            keep.wait()

            @pl.loop(1, 32)
            def _(by):
                row_copy(by, True).wait_recv()

        if name == "w3":
            for which in (0, 1):

                @pl.when(core == which)
                def _():
                    kv_copy(which).start()

        elif name not in pseudo:
            copy_of(by_name[name]).start()

    def finish_message(name):
        if name == "w3":
            i = number["w3"]
            land = k2.at[0, 0, theirs]
            remote(land, land, send.at[i], recv.at[i], across).wait_recv()
        elif name not in pseudo:
            copy_of(by_name[name], True).wait_recv()

    def tables():
        base = chip * 256
        d0 = lax.broadcasted_iota(jnp.int32, (64, 64), 0)
        d1 = lax.broadcasted_iota(jnp.int32, (64, 64), 1)
        spread = jnp.broadcast_to(ln[...].astype(F32), (64, 64))
        end_col = jnp.sum(jnp.where(d1 <= d0, spread, 0.0), axis=1, keepdims=True)
        len_col = jnp.sum(jnp.where(d1 == d0, spread, 0.0), axis=1, keepdims=True)
        end_row = jnp.sum(jnp.where(d0 <= d1, jnp.broadcast_to(len_col, (64, 64)), 0.0), axis=0, keepdims=True)
        row_id = (base + lax.broadcasted_iota(jnp.int32, (64, 256), 1)).astype(F32)
        before = row_id >= end_col
        q_doc = jnp.sum(jnp.where(before, 1.0, 0.0), axis=0, keepdims=True)
        position = row_id - jnp.sum(jnp.where(before, len_col, 0.0), axis=0, keepdims=True)
        turn = lax.broadcasted_iota(jnp.int32, (64, 256), 0).astype(F32)
        angle = position * jnp.exp(turn * (-2.0 / HD * math.log(ROPE_BASE)))
        cs[...] = jnp.transpose(jnp.concatenate([jnp.cos(angle), jnp.sin(angle)], axis=0))
        key_id = base - 384 + lax.broadcasted_iota(jnp.int32, (640, 64), 0)
        k_doc = jnp.sum(jnp.where(key_id.astype(F32) >= end_row, 1.0, 0.0), axis=1, keepdims=True)
        for qb in (0, 1):
            lo = 128 * qb
            kid = base - 384 + lo + lax.broadcasted_iota(jnp.int32, (512, 128), 0)
            qid = base + lo + lax.broadcasted_iota(jnp.int32, (512, 128), 1)
            allowed = (k_doc[lo : lo + 512] == q_doc[:, lo : lo + 128]) & (kid <= qid) & (kid >= 0)
            bias[qb] = jnp.where(allowed, 0.0, -jnp.inf)

    def columns_of(dz):
        zz = lax.rem(z + dz + 8, 8)
        parts = []
        for dy in DY:
            lane = pl.multiple_of((lax.rem(zz, 2) * 4 + lax.rem(y + dy + 4, 4)) * 128, 128)
            parts.append(xs[zz // 2, :, :, pl.ds(lane, 128)].reshape(256, 128))
        return jnp.concatenate(parts, axis=1)

    def project(dz):
        s = ZS[dz]
        lhs = columns_of(dz)
        one = jnp.dot(lhs, q1[s].reshape(512, 256), preferred_element_type=F32)
        two = jnp.dot(lhs, q2[:, s].reshape(512, 256), preferred_element_type=F32)
        if dz == 0:
            acc1[...] = one
            acc2[...] = two
        else:
            acc1[...] += one
            acc2[...] += two

    def turned_pairs():
        table = cs[...]
        swapped = pltpu.roll(table, 64, 1)
        low = lax.broadcasted_iota(jnp.int32, (256, 128), 1) < 64
        return jnp.where(low, table, swapped), jnp.where(low, -swapped, table)

    def rope(e):
        cosine, sine = turned_pairs()
        return e * cosine + pltpu.roll(e, 64, 1) * sine

    def make_kv():
        raw = None
        for dz in DZ:
            term = jnp.dot(columns_of(dz), k2[:, ZS[dz]].reshape(512, 128), preferred_element_type=F32)
            raw = term if raw is None else raw + term
        acck[...] = raw
        raw = acck[...]
        kv[core, 384:640] = jnp.where(core == 0, rope(raw), raw).astype(BF16)

    def rope_queries():
        for h in range(4):
            e = acc1[:, 128 * h : 128 * h + 128] if h < 2 else acc2[:, 128 * (h - 2) : 128 * (h - 2) + 128]
            turned_e = rope(e).astype(BF16)
            for qb in (0, 1):
                qs[qb, h // 2, 128 * (h % 2) : 128 * (h % 2) + 128] = turned_e[128 * qb : 128 * qb + 128]

    def turn_values():
        eye = (
            lax.broadcasted_iota(jnp.int32, (128, 128), 0) == lax.broadcasted_iota(jnp.int32, (128, 128), 1)
        ).astype(F32).astype(BF16)
        vt[...] = lax.dot_general(eye, kv[1], (((1,), (1,)), ((), ())), preferred_element_type=F32).astype(BF16)

    def attend(qb, pair):
        keys = kv[0, 128 * qb : 128 * qb + 512]
        scores = lax.dot_general(keys, qs[qb, pair], (((1,), (1,)), ((), ())), preferred_element_type=F32)
        mask = bias[qb]
        scores = scores * (1.0 / math.sqrt(HD)) + jnp.concatenate([mask, mask], axis=1)
        expo = jnp.exp(scores - jnp.max(scores, axis=0, keepdims=True))
        denominator = jnp.sum(expo, axis=0, keepdims=True)
        summed = jnp.dot(vt[:, 128 * qb : 128 * qb + 512], expo.astype(BF16), preferred_element_type=F32)
        result = (summed / denominator).astype(BF16)
        for h in (0, 1):
            att[core, pair, qb, 128 * h : 128 * h + 128] = result[:, 128 * h : 128 * h + 128]

    def part_copy(dz, which, t, start):
        s = ZS[dz]
        zz = lax.rem(z + dz + 8, 8)
        goal = zz // 2
        here = (goal == x) & (core == t)
        sem = precv.at[core, x, lax.rem(zz, 2), which]
        land = rs.at[core, x, lax.rem(zz, 2), which]

        @pl.when(jnp.logical_not(here))
        def _():
            copy = remote(part.at[s, which, t], land, psend.at[s, which, t], sem, (chip * 2 + t, goal))
            copy.start() if start else copy.wait_send()

        if start:

            @pl.when(here)
            def _():
                pltpu.make_async_copy(part.at[s, which, t], land, sem).start()

    def out_project(dz, which):
        s = ZS[dz]
        dy = slice(2 * which, 2 * which + 2)
        weights = jnp.concatenate([att[:, :, 0].reshape(1024, 128), att[:, :, 1].reshape(1024, 128)], axis=1)
        total = jnp.dot(o1[s, dy].reshape(128, 384), weights[:384], preferred_element_type=F32)
        total += jnp.dot(o2[dy, s].reshape(128, 640), weights[384:], preferred_element_type=F32)
        total = total.astype(BF16)
        for t in (0, 1):
            part[s, which, t] = total[:, 128 * t : 128 * t + 128]
            part_copy(dz, which, t, True)

    def run(name):
        if name == "tables":
            tables()
        elif name == "place":
            place()
        elif name == "kv":
            make_kv()
        elif name == "rope":
            rope_queries()
        elif name == "vt":
            turn_values()
        elif name[0] == "A":
            attend(int(name[1]), int(name[2]))
        elif name[0] == "Q":
            project(int(name[1:]))
        else:
            dz, which = name[1:].split(",")
            out_project(int(dz), int(which))

    for _, _, kind, name in actions:
        if kind == "send":
            start_message(name)
        elif kind == "recv":
            finish_message(name)
        else:
            run(name)

    @pl.loop(1, 32)
    def _(by):
        row_copy(by).wait_send()

    kv_copy(0).wait_send()
    for m in messages:
        if m.name not in pseudo and m.name != "w3":
            copy_of(m).wait_send()
    for late_half in (0, 1):
        zz = lax.rem(z + 1 + late_half, 2)
        sums = []
        for c in (0, 1):
            total = None
            for g in range(4):
                for which in (0, 1):
                    land = rs.at[c, g, zz, which]
                    remote(land, land, psend.at[0, 0, 0], precv.at[c, g, zz, which], across).wait_recv()
                term = rs[c, g, zz].reshape(256, 128).astype(F32)
                total = term if total is None else total + term
            sums.append(total)
        for dy in DY:
            s = YS[dy]
            block = jnp.concatenate([sums[0][64 * s : 64 * s + 64], sums[1][64 * s : 64 * s + 64]], axis=0)
            lane = pl.multiple_of((zz * 4 + lax.rem(y + dy + 4, 4)) * 128, 128)
            out[:, pl.ds(lane, 128)] = jnp.transpose(block).astype(BF16)
    for dz in DZ:
        for which in (0, 1):
            for t in (0, 1):
                part_copy(dz, which, t, False)


def per_device(tokens, context_row, lengths, qw, kw, vw, ow):
    nodes, actions, _ = plan()
    messages = [n for n in nodes if n.link != "core"]
    count = len(messages)
    dma = pltpu.SemaphoreType.DMA
    scratch = [
        pltpu.VMEM((4, 8, 128, 128), BF16),
        pltpu.VMEM((8, 4, 128, 256), BF16),
        pltpu.VMEM((4, 8, 128, 256), BF16),
        pltpu.VMEM((8, 4, 64, 384), BF16),
        pltpu.VMEM((4, 8, 64, 640), BF16),
        pltpu.VMEM((128, 1024), BF16),
        pltpu.VMEM((64, 128), jnp.int32),
        pltpu.VMEM((1, 64), jnp.int32),
        pltpu.VMEM((3072, 128), F32),
        pltpu.VMEM((32, 48, 128), BF16),
        pltpu.VMEM((32, 2, 48, 128), BF16),
        pltpu.VMEM((4, 2, 128, 1024), BF16),
        pltpu.VMEM((256, 128), F32),
        pltpu.VMEM((256, 256), F32),
        pltpu.VMEM((256, 256), F32),
        pltpu.VMEM((256, 128), F32),
        pltpu.VMEM((2, 512, 128), F32),
        pltpu.VMEM((2, 2, 256, 128), BF16),
        pltpu.VMEM((2, 640, 128), BF16),
        pltpu.VMEM((128, 640), BF16),
        pltpu.VMEM((2, 2, 2, 256, 128), BF16),
        pltpu.VMEM((8, 2, 2, 128, 128), BF16),
        pltpu.VMEM((2, 4, 2, 2, 128, 128), BF16),
        dma((9,)),
        dma((count,)),
        dma((count,)),
        dma((32,)),
        dma((32,)),
        dma((8, 2, 2)),
        dma((2, 4, 2, 2)),
    ]

    def body(*refs):
        kernel(messages, actions, *refs)

    return pl.pallas_call(
        body,
        out_shape=pltpu.VMEM((128, 1024), BF16),
        in_specs=[pl.BlockSpec(memory_space=pltpu.HBM)] * 7,
        out_specs=pl.BlockSpec(memory_space=pltpu.VMEM),
        scratch_shapes=scratch,
        compiler_params=pltpu.CompilerParams(
            collective_id=0, has_side_effects=True, vmem_limit_bytes=63 * 2**20
        ),
    )(tokens, context_row.reshape(64, 128), lengths.reshape(1, 64), qw, kw, vw, ow.T)


def solution(mesh):
    return jax.shard_map(
        per_device,
        mesh=mesh,
        in_specs=(
            P("ctx", "head"),
            P(),
            P(),
            P("ctx", "head"),
            P("ctx", "head"),
            P("ctx", "head"),
            P("head", "ctx"),
        ),
        out_specs=P("ctx", "head"),
        check_vma=False,
    )
```

```python
import math

import jax
import jax.numpy as jnp
from jax import lax
from jax.experimental import pallas as pl
from jax.experimental.pallas import tpu as pltpu
from jax.sharding import PartitionSpec as P

MESH = pl.DeviceIdType.MESH
F32 = jnp.float32
BF16 = jnp.bfloat16
ROPE_BASE = 500000.0
HD = 128

DZ = (0, 1, -1, 2, -2, 3, -3, 4)
DY = (0, 1, -1, 2)
ZS = {d: i for i, d in enumerate(DZ)}
YS = {d: i for i, d in enumerate(DY)}
GROUPS = ((0, 1), (1, 3), (3, 5), (5, 7), (7, 8))
WIDE_GROUPS = ((0, 3), (3, 7), (7, 8))

LINK_RATE, LINK_LATENCY = 44, 3.2
PEER_RATE, PEER_LATENCY = 400.0, 1.0
AHEAD = 2.0
EXTRA = {"r": 6.0, "x": 1.0, "h": 1.0, "a": 0.5}


class Node:
    def __init__(self, name, link, deps, size, prio=(0,), src=None, dst=None):
        self.name, self.link, self.deps, self.size, self.prio = name, link, deps, size, prio
        self.src, self.dst = src, dst


def gather_messages(tag, rows, width1, width2, ready, rank, groups=GROUPS):
    out = []
    half = rows // 2
    size1 = rows * width1 * 2e-3
    size2 = rows * width2 * 2e-3
    full, top, bottom = (0, rows), (0, half), (half, half)

    def one(dz, dy, part):
        return (tag + "1", ZS[dz], YS[dy], part)

    def pair(dz, which):
        return (tag + "1", ZS[dz], (2 * which, 2), full)

    def two(dy, dz, part):
        return (tag + "2", YS[dy], ZS[dz], part)

    def group(dy, g):
        lo, hi = groups[g]
        return (tag + "2", YS[dy], (lo, hi - lo), full)

    def add(name, link, src, dst, deps, size, prio):
        out.append(Node(tag + name, link, [tag + d for d in deps] + ready, size, (rank,) + prio, src, dst))

    if width1:
        add("1y+1", "+y", one(0, 0, full), one(0, -1, full), [], size1, (0, 1))
        add("1y-1", "-y", one(0, 0, full), one(0, 1, full), [], size1, (0, 1))
        add("1y+2", "+y", one(0, -1, top), one(0, 2, top), ["1y+1"], size1 / 2, (0, 2))
        add("1y-2", "-y", one(0, 1, bottom), one(0, 2, bottom), ["1y-1"], size1 / 2, (0, 2))
    first = {0: ["1y-1"], 1: ["1y+1", "1y+2", "1y-2"]}
    for which in (0, 1) if width1 else ():
        for sign, link in ((1, "+z"), (-1, "-z")):
            mark = "+" if sign > 0 else "-"
            for step in (1, 2, 3, 4):
                if step == 4 and (sign > 0) != (which == 0):
                    continue
                deps = first[which] if step == 1 else [f"1z{which}{mark}{step - 1}"]
                far = 4 if step == 4 else -sign * step
                add(f"1z{which}{mark}{step}", link, pair(-sign * (step - 1), which), pair(far, which), deps,
                    2 * size1, (1, step))
    for sign, link in ((1, "+z"), (-1, "-z")):
        mark = "+" if sign > 0 else "-"
        for step in (1, 2, 3, 4):
            deps = [] if step == 1 else [f"2z{mark}{step - 1}"]
            part = full if step < 4 else (top if sign > 0 else bottom)
            far = 4 if step == 4 else -sign * step
            add(f"2z{mark}{step}", link, two(0, -sign * (step - 1), part), two(0, far, part), deps,
                size2 if step < 4 else size2 / 2, (0, step))
    for g, (lo, hi) in enumerate(groups):
        deps = []
        for dz in DZ[lo:hi]:
            deps += z_messages(dz)
        amount = size2 * (hi - lo)
        add(f"2y{g}+1", "+y", group(0, g), group(-1, g), deps, amount, (1, g))
        add(f"2y{g}-1", "-y", group(0, g), group(1, g), deps, amount, (1, g))
        if g % 2 == 0:
            add(f"2y{g}+2", "+y", group(-1, g), group(2, g), [f"2y{g}+1"], amount, (1, g))
        else:
            add(f"2y{g}-2", "-y", group(1, g), group(2, g), [f"2y{g}-1"], amount, (1, g))
    return out


def z_messages(dz):
    if dz == 0:
        return []
    return ["2z+4", "2z-4"] if dz == 4 else [f"2z{'+' if dz < 0 else '-'}{abs(dz)}"]


def needs(tag, dz, which, groups=GROUPS):
    g = [i for i, (lo, hi) in enumerate(groups) if lo <= ZS[dz] < hi][0]
    if which == 0:
        names = z_messages(dz) + [f"2y{g}-1"]
    else:
        names = [f"2y{g}+1", f"2y{g}+2" if g % 2 == 0 else f"2y{g}-2"]
    if tag != "k":
        if dz == 0:
            names += ["1y-1"] if which == 0 else ["1y+1", "1y+2", "1y-2"]
        elif dz == 4:
            names += ["1z0+4"] if which == 0 else ["1z1-4"]
        else:
            names += [f"1z{which}{'+' if dz < 0 else '-'}{abs(dz)}"]
    return [tag + n for n in names]


def all_nodes():
    x_all = ["x+a", "x+b", "x-a", "x-b", "xs+", "xs-", "xs2"]
    nodes = [
        Node("w1", "peer", [], 33),
        Node("w2", "peer", [], 33),
        Node("w3", "peer", [], 17),
        Node("r+z", "+z", [], 384, (-2,)),
        Node("r-z", "-z", [], 384, (-2,)),
        Node("r+y", "+y", [], 192, (-2,)),
        Node("r-y", "-y", [], 192, (-2,)),
        Node("rows", "peer", ["r+z", "r-z", "r+y", "r-y"], 384, (-1,)),
        Node("x+a", "+x", ["place"], 131, (0, 0)),
        Node("x+b", "+x", ["place"], 131, (0, 1)),
        Node("x-b", "-x", ["place"], 131, (0, 0)),
        Node("x-a", "-x", ["place"], 131, (0, 1)),
        Node("x+2", "+x", ["x+a"], 131, (0, 2)),
        Node("x-2", "-x", ["x-b"], 131, (0, 2)),
        Node("xs+", "peer", ["x+a", "x+b"], 262, (1,)),
        Node("xs-", "peer", ["x-a", "x-b"], 262, (1,)),
        Node("xs2", "peer", ["x+2", "x-2"], 262, (1,)),
        Node("h0", "peer", ["kv"], 65, (0,)),
        Node("h1", "+y", ["kv"], 85, (-1, 0)),
        Node("h2", "+y", ["kv"], 65, (-1, 1)),
        Node("h1s", "peer", ["h1"], 65, (0,)),
        Node("h2s", "peer", ["h2"], 33, (0,)),
    ]
    nodes += gather_messages("k", 128, 0, 128, ["w3"], 0, WIDE_GROUPS)
    nodes += gather_messages("q", 128, 256, 256, ["w1", "w2"], 1)
    nodes += gather_messages("o", 64, 384, 640, [], 2)

    def step(name, deps, span):
        nodes.append(Node(name, "core", deps, span, (len(nodes),)))

    step("tables", [], 1.5)
    step("place", ["rows"], 1.3)
    every = [n for dz in DZ for which in (0, 1) for n in needs("k", dz, which, WIDE_GROUPS)]
    step("kv", every + x_all + ["tables"], 1.0)
    for dz in DZ:
        step(f"Q{dz}", needs("q", dz, 0) + needs("q", dz, 1) + x_all, 0.45)
    step("rope", [f"Q{dz}" for dz in DZ] + ["tables"], 0.6)
    step("vt", ["h0", "h1", "h2", "h1s", "h2s"], 0.2)
    for qb in (0, 1):
        for pair in (0, 1):
            step(f"A{qb}{pair}", ["rope", "vt"], 0.8)
            nodes.append(Node(f"a{qb}{pair}", "peer", [f"A{qb}{pair}"], 65))
    for dz in DZ:
        for which in (0, 1):
            step(f"O{dz},{which}", needs("o", dz, which) + [f"a{qb}{pair}" for qb in (0, 1) for pair in (0, 1)], 0.3)
    return nodes


def plan():
    nodes = all_nodes()
    free, arrival, actions = {}, {}, []
    pending = list(nodes)
    while pending:
        best = None
        by_link = {}
        for m in pending:
            if all(d in arrival for d in m.deps):
                at = max([arrival[d] for d in m.deps], default=0.0)
                by_link.setdefault(m.link, []).append((at, m))
        for link, options in by_link.items():
            begin = max(free.get(link, 0.0), min(at for at, _ in options))
            at, m = min(((at, m) for at, m in options if at <= begin), key=lambda p: p[1].prio)
            if best is None or begin < best[0]:
                best = (begin, m, at)
        begin, m, at = best
        if m.link == "core":
            span, latency = m.size, 0.0
        elif m.link == "peer":
            span, latency = m.size / PEER_RATE, PEER_LATENCY
        else:
            span, latency = m.size / LINK_RATE, LINK_LATENCY
        latency += EXTRA.get(m.name[0], 0.0) if m.link != "core" and m.name != "rows" else 0.0
        free[m.link] = begin + span
        arrival[m.name] = begin + span + latency
        pending.remove(m)
        if m.link == "core":
            actions.append((begin, 2, "step", m.name))
        else:
            actions.append((max(at, begin - AHEAD), 1, "send", m.name))
            actions.append((arrival[m.name], 0, "recv", m.name))
    actions.sort(key=lambda a: a[:2])
    return nodes, actions, arrival


def kernel(messages, actions, tokens, table, lens, qw, kw, vw, ow, out,
           k2, q1, q2, o1, o2, tk, tb, ln, wide, rows_out, rows_in, xs, acck, acc1, acc2, cs, bias, qs, kv, vt, att, part, rs,
           lsem, send, recv, rsend, rrecv, psend, precv):
    ctx, x = lax.axis_index("ctx"), lax.axis_index("head")
    z, y, core = ctx // 8, (ctx // 2) % 4, ctx % 2
    chip = ctx // 2
    other = 1 - core
    buffers = {"k2": k2, "q1": q1, "q2": q2, "o1": o1, "o2": o2}
    number = {m.name: i for i, m in enumerate(messages)}

    def at(dz, dy, which, dx=0):
        return ((lax.rem(z + dz + 8, 8) * 4 + lax.rem(y + dy + 4, 4)) * 2 + which, lax.rem(x + dx + 4, 4))

    def chip_at(by, which):
        return (lax.rem(chip + by + 32, 32) * 2 + which, x)

    across = at(0, 0, other)
    mine = pl.ds(pl.multiple_of(core * 64, 64), 64)
    theirs = pl.ds(pl.multiple_of(other * 64, 64), 64)

    def columns(which, part):
        lo, n = ((0, 256), (256, 256))[part]
        return pl.ds(pl.multiple_of(which * 512 + lo, 128), n)

    def local(i, src, dst):
        return pltpu.make_async_copy(src, dst, lsem.at[i])

    own_kv = [local(7, kw, k2.at[0, 0, mine]), local(7, vw, k2.at[0, 0, mine])]
    early = [local(0, tokens, tk), local(1, table, tb), local(2, lens, ln)]
    late = [
        local(3, qw.at[:, columns(core, 0)], q1.at[0, 0, mine]),
        local(4, qw.at[:, columns(core, 1)], q2.at[0, 0, mine]),
        local(5, ow.at[:, pl.ds(0, 384)], o1.at[0, 0]),
        local(6, ow.at[:, pl.ds(384, 640)], o2.at[0, 0]),
    ]
    peers = [across] + [at(0, 0, which, dx) for dx in (1, 2, 3) for which in (0, 1)]
    peers += [chip_at(by, other) for by in (1, 2, -1, -2)]
    barrier = pltpu.get_barrier_semaphore()
    for peer in peers:
        pl.semaphore_signal(barrier, inc=1, device_id=peer, device_id_type=MESH)

    @pl.loop(1, 32)
    def _(by):
        pl.semaphore_signal(barrier, inc=1, device_id=chip_at(by, core), device_id_type=MESH)

    for copy in early + late:
        copy.start()
    for which in (0, 1):

        @pl.when(core == which)
        def _():
            own_kv[which].start()

    for copy in early:
        copy.wait()
    i0 = lax.broadcasted_iota(jnp.int32, (128, 128), 0)
    i1 = lax.broadcasted_iota(jnp.int32, (128, 128), 1)
    goal_row = jnp.broadcast_to((tb[pl.ds(ctx, 1), :] >> 7).astype(F32), (128, 128))
    goal_col = jnp.sum(jnp.where(i0 == i1, goal_row, 0.0), axis=1, keepdims=True)
    rank = jnp.sum(jnp.where((goal_col == goal_row) & (i0 < i1), 1.0, 0.0), axis=0, keepdims=True)
    slot = 3.0 * goal_row[:1] + rank
    pick = jnp.where(lax.broadcasted_iota(jnp.int32, (192, 128), 0).astype(F32) == slot, 1.0, 0.0).astype(BF16)
    picked = jnp.dot(pick, tk[...], preferred_element_type=F32)
    for j in range(8):
        wide[pl.ds(j, 192, stride=8), :] = picked[:, 128 * j : 128 * j + 128]
    rows_out[...] = wide[0:1536, :].astype(BF16).reshape(32, 48, 128)
    pl.semaphore_wait(barrier, len(peers) + 31)

    def row_copy(by, coming=False):
        goal, origin = lax.rem(chip + by, 32), lax.rem(chip + 32 - by, 32)
        src, dst = rows_out.at[goal], rows_in.at[chip, core]
        if coming:
            src = dst = rows_in.at[origin, core]
        return pltpu.make_async_remote_copy(
            src_ref=src, dst_ref=dst, send_sem=rsend.at[by], recv_sem=rrecv.at[by],
            device_id=chip_at(by, core), device_id_type=MESH,
        )

    @pl.loop(0, 31)
    def _(i):
        row_copy(1 + lax.rem(i + 15, 31)).start()

    keep = local(8, rows_out.at[chip], rows_in.at[chip, core])
    keep.start()
    for copy in late:
        copy.wait()
    own_kv[0].wait()

    x_low, x_high, x_far = lax.rem(x + 3, 4), lax.rem(x + 1, 4), lax.rem(x + 2, 4)
    top, bottom = pl.ds(0, 64), pl.ds(64, 64)
    far_keys, near_keys, own_keys, upper_keys = pl.ds(0, 128), pl.ds(128, 256), pl.ds(384, 256), pl.ds(512, 128)
    special = {
        "w1": (qw.at[:, columns(other, 0)], q1.at[0, 0, mine], q1.at[0, 0, theirs], across),
        "w2": (qw.at[:, columns(other, 1)], q2.at[0, 0, mine], q2.at[0, 0, theirs], across),
        "rows": (rows_in.at[:, core], rows_in.at[:, core], rows_in.at[:, other], across),
        "x+a": (xs.at[x, core, top], xs.at[x, core, top], xs.at[x_low, core, top], at(0, 0, core, 1)),
        "x+b": (xs.at[x, core, bottom], xs.at[x, core, bottom], xs.at[x_low, core, bottom], at(0, 0, core, 1)),
        "x-a": (xs.at[x, core, top], xs.at[x, core, top], xs.at[x_high, core, top], at(0, 0, core, -1)),
        "x-b": (xs.at[x, core, bottom], xs.at[x, core, bottom], xs.at[x_high, core, bottom], at(0, 0, core, -1)),
        "x+2": (xs.at[x_low, core, top], xs.at[x_low, core, top], xs.at[x_far, core, top], at(0, 0, core, 1)),
        "x-2": (xs.at[x_high, core, bottom], xs.at[x_high, core, bottom], xs.at[x_far, core, bottom],
                at(0, 0, core, -1)),
        "xs+": (xs.at[x_low, core], xs.at[x_low, core], xs.at[x_low, other], across),
        "xs-": (xs.at[x_high, core], xs.at[x_high, core], xs.at[x_high, other], across),
        "xs2": (xs.at[x_far, core], xs.at[x_far, core], xs.at[x_far, other], across),
        "h0": (kv.at[core, own_keys], kv.at[core, own_keys], kv.at[other, own_keys], across),
        "h1": (kv.at[core, own_keys], kv.at[core, near_keys], kv.at[core, near_keys], chip_at(1, core)),
        "h2": (kv.at[core, upper_keys], kv.at[core, far_keys], kv.at[core, far_keys], chip_at(2, core)),
        "h1s": (kv.at[core, near_keys], kv.at[core, near_keys], kv.at[other, near_keys], across),
        "h2s": (kv.at[core, far_keys], kv.at[core, far_keys], kv.at[other, far_keys], across),
    }
    for qb in (0, 1):
        for pair in (0, 1):
            special[f"a{qb}{pair}"] = (att.at[core, pair, qb], att.at[core, pair, qb], att.at[other, pair, qb], across)
    to = {"+z": at(1, 0, core), "-z": at(-1, 0, core), "+y": at(0, 1, core), "-y": at(0, -1, core)}

    def view(place):
        name, a, b, (lo, n) = place
        b = pl.ds(*b) if isinstance(b, tuple) else b
        return buffers[name].at[a, b, pl.ds(lo, n)]

    def remote(src, dst, ssem, rsem, device):
        return pltpu.make_async_remote_copy(
            src_ref=src, dst_ref=dst, send_sem=ssem, recv_sem=rsem, device_id=device, device_id_type=MESH
        )

    def copy_of(m, coming=False):
        i = number[m.name]
        if m.name in special:
            src, dst, land, device = special[m.name]
        else:
            src, dst, land, device = view(m.src), view(m.dst), view(m.dst), to[m.link]
        if coming:
            src = dst = land
        return remote(src, dst, send.at[i], recv.at[i], device)

    by_name = {m.name: m for m in messages}

    def kv_copy(which):
        i = number["w3"]
        src = (vw, kw)[which]
        return remote(src, k2.at[0, 0, mine], send.at[i], recv.at[i], across)

    def place():
        t = tb[...]
        upper = jnp.where(i0 < i1, 1.0, 0.0).astype(BF16)
        landing = []
        for half in (0, 1):
            here = (t >> 7) == 2 * chip + half
            nth = jnp.dot(jnp.where(here, 1.0, 0.0).astype(BF16), upper, preferred_element_type=F32)
            row = ((t & 255) + 1).astype(F32)
            for k in range(3):
                landing.append(jnp.sum(jnp.where(here & (nth == float(k)), row, 0.0), axis=1, keepdims=True))
        goal = jnp.concatenate(landing, axis=0)
        lane = lax.broadcasted_iota(jnp.int32, (384, 256), 1).astype(F32) + 1.0
        spot = jnp.transpose(jnp.where(goal == lane, 1.0, 0.0)).astype(BF16)
        wide[...] = rows_in[...].astype(F32).reshape(3072, 128)
        for j in range(8):
            rows = [wide[pl.ds(8 * n + j, 64, stride=48), :] for n in range(6)]
            rows = jnp.concatenate(rows, axis=0).astype(BF16)
            found = jnp.dot(spot, rows, preferred_element_type=F32).astype(BF16)
            xs[x, :, :, 128 * j : 128 * j + 128] = found.reshape(2, 128, 128)

    pseudo = ("r+z", "r-z", "r+y", "r-y")

    def start_message(name):
        if name == "rows":
            keep.wait()

            @pl.loop(1, 32)
            def _(by):
                row_copy(by, True).wait_recv()

        if name == "w3":
            for which in (0, 1):

                @pl.when(core == which)
                def _():
                    kv_copy(which).start()

        elif name not in pseudo:
            copy_of(by_name[name]).start()

    def finish_message(name):
        if name == "w3":
            i = number["w3"]
            land = k2.at[0, 0, theirs]
            remote(land, land, send.at[i], recv.at[i], across).wait_recv()
        elif name not in pseudo:
            copy_of(by_name[name], True).wait_recv()

    def tables():
        base = chip * 256
        d0 = lax.broadcasted_iota(jnp.int32, (64, 64), 0)
        d1 = lax.broadcasted_iota(jnp.int32, (64, 64), 1)
        spread = jnp.broadcast_to(ln[...].astype(F32), (64, 64))
        end_col = jnp.sum(jnp.where(d1 <= d0, spread, 0.0), axis=1, keepdims=True)
        len_col = jnp.sum(jnp.where(d1 == d0, spread, 0.0), axis=1, keepdims=True)
        end_row = jnp.sum(jnp.where(d0 <= d1, jnp.broadcast_to(len_col, (64, 64)), 0.0), axis=0, keepdims=True)
        row_id = (base + lax.broadcasted_iota(jnp.int32, (64, 256), 1)).astype(F32)
        before = row_id >= end_col
        q_doc = jnp.sum(jnp.where(before, 1.0, 0.0), axis=0, keepdims=True)
        position = row_id - jnp.sum(jnp.where(before, len_col, 0.0), axis=0, keepdims=True)
        turn = lax.broadcasted_iota(jnp.int32, (64, 256), 0).astype(F32)
        angle = position * jnp.exp(turn * (-2.0 / HD * math.log(ROPE_BASE)))
        cs[...] = jnp.transpose(jnp.concatenate([jnp.cos(angle), jnp.sin(angle)], axis=0))
        key_id = base - 384 + lax.broadcasted_iota(jnp.int32, (640, 64), 0)
        k_doc = jnp.sum(jnp.where(key_id.astype(F32) >= end_row, 1.0, 0.0), axis=1, keepdims=True)
        for qb in (0, 1):
            lo = 128 * qb
            kid = base - 384 + lo + lax.broadcasted_iota(jnp.int32, (512, 128), 0)
            qid = base + lo + lax.broadcasted_iota(jnp.int32, (512, 128), 1)
            allowed = (k_doc[lo : lo + 512] == q_doc[:, lo : lo + 128]) & (kid <= qid) & (kid >= 0)
            bias[qb] = jnp.where(allowed, 0.0, -jnp.inf)

    def columns_of(dz):
        zz = lax.rem(z + dz + 8, 8)
        parts = []
        for dy in DY:
            lane = pl.multiple_of((lax.rem(zz, 2) * 4 + lax.rem(y + dy + 4, 4)) * 128, 128)
            parts.append(xs[zz // 2, :, :, pl.ds(lane, 128)].reshape(256, 128))
        return jnp.concatenate(parts, axis=1)

    def project(dz):
        s = ZS[dz]
        lhs = columns_of(dz)
        one = jnp.dot(lhs, q1[s].reshape(512, 256), preferred_element_type=F32)
        two = jnp.dot(lhs, q2[:, s].reshape(512, 256), preferred_element_type=F32)
        if dz == 0:
            acc1[...] = one
            acc2[...] = two
        else:
            acc1[...] += one
            acc2[...] += two

    def turned_pairs():
        table = cs[...]
        swapped = pltpu.roll(table, 64, 1)
        low = lax.broadcasted_iota(jnp.int32, (256, 128), 1) < 64
        return jnp.where(low, table, swapped), jnp.where(low, -swapped, table)

    def rope(e):
        cosine, sine = turned_pairs()
        return e * cosine + pltpu.roll(e, 64, 1) * sine

    def make_kv():
        raw = None
        for dz in DZ:
            term = jnp.dot(columns_of(dz), k2[:, ZS[dz]].reshape(512, 128), preferred_element_type=F32)
            raw = term if raw is None else raw + term
        acck[...] = raw
        raw = acck[...]
        kv[core, 384:640] = jnp.where(core == 0, rope(raw), raw).astype(BF16)

    def rope_queries():
        for h in range(4):
            e = acc1[:, 128 * h : 128 * h + 128] if h < 2 else acc2[:, 128 * (h - 2) : 128 * (h - 2) + 128]
            turned_e = rope(e).astype(BF16)
            for qb in (0, 1):
                qs[qb, h // 2, 128 * (h % 2) : 128 * (h % 2) + 128] = turned_e[128 * qb : 128 * qb + 128]

    def turn_values():
        eye = (
            lax.broadcasted_iota(jnp.int32, (128, 128), 0) == lax.broadcasted_iota(jnp.int32, (128, 128), 1)
        ).astype(F32).astype(BF16)
        vt[...] = lax.dot_general(eye, kv[1], (((1,), (1,)), ((), ())), preferred_element_type=F32).astype(BF16)

    def attend(qb, pair):
        keys = kv[0, 128 * qb : 128 * qb + 512]
        scores = lax.dot_general(keys, qs[qb, pair], (((1,), (1,)), ((), ())), preferred_element_type=F32)
        mask = bias[qb]
        scores = scores * (1.0 / math.sqrt(HD)) + jnp.concatenate([mask, mask], axis=1)
        expo = jnp.exp(scores - jnp.max(scores, axis=0, keepdims=True))
        denominator = jnp.sum(expo, axis=0, keepdims=True)
        summed = jnp.dot(vt[:, 128 * qb : 128 * qb + 512], expo.astype(BF16), preferred_element_type=F32)
        result = (summed / denominator).astype(BF16)
        for h in (0, 1):
            att[core, pair, qb, 128 * h : 128 * h + 128] = result[:, 128 * h : 128 * h + 128]

    def part_copy(dz, which, t, start):
        s = ZS[dz]
        zz = lax.rem(z + dz + 8, 8)
        goal = zz // 2
        here = (goal == x) & (core == t)
        sem = precv.at[core, x, lax.rem(zz, 2), which]
        land = rs.at[core, x, lax.rem(zz, 2), which]

        @pl.when(jnp.logical_not(here))
        def _():
            copy = remote(part.at[s, which, t], land, psend.at[s, which, t], sem, (chip * 2 + t, goal))
            copy.start() if start else copy.wait_send()

        if start:

            @pl.when(here)
            def _():
                pltpu.make_async_copy(part.at[s, which, t], land, sem).start()

    def out_project(dz, which):
        s = ZS[dz]
        dy = slice(2 * which, 2 * which + 2)
        weights = jnp.concatenate([att[:, :, 0].reshape(1024, 128), att[:, :, 1].reshape(1024, 128)], axis=1)
        total = jnp.dot(o1[s, dy].reshape(128, 384), weights[:384], preferred_element_type=F32)
        total += jnp.dot(o2[dy, s].reshape(128, 640), weights[384:], preferred_element_type=F32)
        total = total.astype(BF16)
        for t in (0, 1):
            part[s, which, t] = total[:, 128 * t : 128 * t + 128]
            part_copy(dz, which, t, True)

    def run(name):
        if name == "tables":
            tables()
        elif name == "place":
            place()
        elif name == "kv":
            make_kv()
        elif name == "rope":
            rope_queries()
        elif name == "vt":
            turn_values()
        elif name[0] == "A":
            attend(int(name[1]), int(name[2]))
        elif name[0] == "Q":
            project(int(name[1:]))
        else:
            dz, which = name[1:].split(",")
            out_project(int(dz), int(which))

    for _, _, kind, name in actions:
        if kind == "send":
            start_message(name)
        elif kind == "recv":
            finish_message(name)
        else:
            run(name)

    @pl.loop(1, 32)
    def _(by):
        row_copy(by).wait_send()

    kv_copy(0).wait_send()
    for m in messages:
        if m.name not in pseudo and m.name != "w3":
            copy_of(m).wait_send()
    for late_half in (0, 1):
        zz = lax.rem(z + 1 + late_half, 2)
        sums = []
        for c in (0, 1):
            total = None
            for g in range(4):
                for which in (0, 1):
                    land = rs.at[c, g, zz, which]
                    remote(land, land, psend.at[0, 0, 0], precv.at[c, g, zz, which], across).wait_recv()
                term = rs[c, g, zz].reshape(256, 128).astype(F32)
                total = term if total is None else total + term
            sums.append(total)
        for dy in DY:
            s = YS[dy]
            block = jnp.concatenate([sums[0][64 * s : 64 * s + 64], sums[1][64 * s : 64 * s + 64]], axis=0)
            lane = pl.multiple_of((zz * 4 + lax.rem(y + dy + 4, 4)) * 128, 128)
            out[:, pl.ds(lane, 128)] = jnp.transpose(block).astype(BF16)
    for dz in DZ:
        for which in (0, 1):
            for t in (0, 1):
                part_copy(dz, which, t, False)


def per_device(tokens, context_row, lengths, qw, kw, vw, ow):
    nodes, actions, _ = plan()
    messages = [n for n in nodes if n.link != "core"]
    count = len(messages)
    dma = pltpu.SemaphoreType.DMA
    scratch = [
        pltpu.VMEM((4, 8, 128, 128), BF16),
        pltpu.VMEM((8, 4, 128, 256), BF16),
        pltpu.VMEM((4, 8, 128, 256), BF16),
        pltpu.VMEM((8, 4, 64, 384), BF16),
        pltpu.VMEM((4, 8, 64, 640), BF16),
        pltpu.VMEM((128, 1024), BF16),
        pltpu.VMEM((64, 128), jnp.int32),
        pltpu.VMEM((1, 64), jnp.int32),
        pltpu.VMEM((3072, 128), F32),
        pltpu.VMEM((32, 48, 128), BF16),
        pltpu.VMEM((32, 2, 48, 128), BF16),
        pltpu.VMEM((4, 2, 128, 1024), BF16),
        pltpu.VMEM((256, 128), F32),
        pltpu.VMEM((256, 256), F32),
        pltpu.VMEM((256, 256), F32),
        pltpu.VMEM((256, 128), F32),
        pltpu.VMEM((2, 512, 128), F32),
        pltpu.VMEM((2, 2, 256, 128), BF16),
        pltpu.VMEM((2, 640, 128), BF16),
        pltpu.VMEM((128, 640), BF16),
        pltpu.VMEM((2, 2, 2, 256, 128), BF16),
        pltpu.VMEM((8, 2, 2, 128, 128), BF16),
        pltpu.VMEM((2, 4, 2, 2, 128, 128), BF16),
        dma((9,)),
        dma((count,)),
        dma((count,)),
        dma((32,)),
        dma((32,)),
        dma((8, 2, 2)),
        dma((2, 4, 2, 2)),
    ]

    def body(*refs):
        kernel(messages, actions, *refs)

    return pl.pallas_call(
        body,
        out_shape=pltpu.VMEM((128, 1024), BF16),
        in_specs=[pl.BlockSpec(memory_space=pltpu.HBM)] * 7,
        out_specs=pl.BlockSpec(memory_space=pltpu.VMEM),
        scratch_shapes=scratch,
        compiler_params=pltpu.CompilerParams(
            collective_id=0, has_side_effects=True, vmem_limit_bytes=63 * 2**20
        ),
    )(tokens, context_row.reshape(64, 128), lengths.reshape(1, 64), qw, kw, vw, ow.T)


def solution(mesh):
    return jax.shard_map(
        per_device,
        mesh=mesh,
        in_specs=(
            P("ctx", "head"),
            P(),
            P(),
            P("ctx", "head"),
            P("ctx", "head"),
            P("ctx", "head"),
            P("head", "ctx"),
        ),
        out_specs=P("ctx", "head"),
        check_vma=False,
    )
```
